32 devices in a mesh: row: 4 (over y, core), col: 8 (over z, x).
Axes of the slice: x: 2, y: 2, z: 4, core: 2. Of those that a mesh axis runs over, the one named last changes fastest.
Arguments:
- points: float32 [3, 65536], P(None, ('row', 'col')), as said below
- values: float32 [16, 65536], P(None, ('row', 'col'))
- tile_lists: int32 [3, 1536], P(None, ('row', 'col')), may hold values from 0 to 63, as said below
Outputs:
- solution: float32 [16, 65536], P(None, ('row', 'col'))
- residual: float32 [16, 65536], P(None, ('row', 'col'))
The draws below stay inside these ranges and needn't reach their ends.
Inputs may be any that keep to these rules, and one draw needn't show every extreme that they name: `tile_lists`: on every device the live slots come first and the rest hold 0, 0, 0; a device holds at most 48 live slots and some device holds exactly that many; no unordered pair of blocks is listed twice, in either order. Block pairs whose points can come within the support radius are listed. Coordinates of point blocks that lie in cells of a square lattice of unit cells, 256 points to a block.
All inputs are finite; a program needn't handle non-finite values.
Results may differ from the reference program's by a relative error of at most 0.0003.
Values sent between devices are 32-bit elements; how exact they have to be, the bound alone decides.
No kernel may reach another device: no remote copies, remote signals or barrier semaphores. Data moves between devices by JAX's collectives and lax.ppermute only.
A program may use at most 64 MiB of HBM per device.

```python
import jax
import jax.numpy as jnp
from jax import lax

BLK = 256
BPD = 8
NRHS = 16
ITERS = 2
TILES_DEV = 48
NBLK = 256
NPTS = 65536
N_ROW = 4
N_COL = 8


def split_code(morton):
    cell_x = jnp.zeros_like(morton)
    cell_y = jnp.zeros_like(morton)
    for level in range(12):
        cell_x = cell_x + morton // 4 ** level % 2 * 2 ** level
        cell_y = cell_y + morton // (2 * 4 ** level) % 2 * 2 ** level
    return (cell_x, cell_y)


def join_code(cell_x, cell_y):
    morton = jnp.zeros_like(cell_x)
    for level in range(12):
        morton = morton + cell_x // 2 ** level % 2 * 4 ** level
        morton = morton + cell_y // 2 ** level % 2 * (2 * 4 ** level)
    return morton


def occupied(key):
    cell_total = 2 * NBLK
    shuffled = jax.random.permutation(jax.random.fold_in(key, 11), cell_total)
    return jnp.sort(shuffled[:NBLK]).astype(jnp.int32)


def draw_points(key, part):
    cell_x, cell_y = split_code(occupied(key))
    corner = jnp.stack([cell_x, cell_y, jnp.zeros_like(cell_x)]).astype(jnp.float32)
    jitter = jax.random.uniform(jax.random.fold_in(key, 21), (3, NBLK, BLK), jnp.float32)
    spread = jnp.array([1.0, 1.0, 0.3], jnp.float32)
    lowest = jnp.array([0.0, 0.0, -0.15], jnp.float32)
    placed = corner[:, :, None] + jitter * spread[:, None, None] + lowest[:, None, None]
    return placed.reshape(3, NPTS)


def draw_values(key, part):
    position = jnp.arange(NPTS, dtype=jnp.float32) / NPTS
    field_gain = jnp.exp(jax.random.uniform(jax.random.fold_in(key, 5), (NRHS, 1), jnp.float32, -0.7, 0.7))
    noise = jax.random.normal(jax.random.fold_in(key, 6), (NRHS, NPTS), jnp.float32)
    rising = 0.6 * jnp.power(3.0, position)
    return noise * rising[None, :] * field_gain


def draw_tile_lists(key, part):
    morton = occupied(key)
    cell_total = 2 * NBLK
    devices = N_ROW * N_COL
    row_span = N_COL * BPD
    col_span = N_ROW * BPD
    slot_total = devices * TILES_DEV
    lookup = jnp.full((cell_total,), -1, jnp.int32).at[morton].set(jnp.arange(NBLK, dtype=jnp.int32))
    cell_x, cell_y = split_code(morton)
    step_x = jnp.array([-1, -1, -1, 0, 0, 0, 1, 1, 1], jnp.int32)
    step_y = jnp.array([-1, 0, 1, -1, 0, 1, -1, 0, 1], jnp.int32)
    near_x = cell_x[:, None] + step_x[None, :]
    near_y = cell_y[:, None] + step_y[None, :]
    near_code = join_code(jnp.maximum(near_x, 0), jnp.maximum(near_y, 0))
    inside = (near_x >= 0) & (near_y >= 0) & (near_code < cell_total)
    partner = jnp.where(inside, lookup[jnp.minimum(near_code, cell_total - 1)], -1)
    own_block = jnp.broadcast_to(jnp.arange(NBLK, dtype=jnp.int32)[:, None], (NBLK, 9))
    usable = (partner >= own_block).reshape(-1)
    lower_block = own_block.reshape(-1)
    upper_block = jnp.maximum(partner.reshape(-1), 0)
    flip = jax.random.randint(jax.random.fold_in(key, 51), (NBLK * 9,), 0, 2)
    row_block = jnp.where(flip == 1, upper_block, lower_block)
    col_block = jnp.where(flip == 1, lower_block, upper_block)
    owner = row_block // row_span * N_COL + col_block // BPD % N_COL
    keyed = jnp.where(usable, owner, devices).astype(jnp.int32)
    order = jnp.argsort(keyed, stable=True)
    sorted_key = keyed[order]
    starts = jnp.searchsorted(sorted_key, jnp.arange(devices + 1, dtype=jnp.int32)).astype(jnp.int32)
    rank_in = jnp.arange(sorted_key.shape[0], dtype=jnp.int32) - starts[sorted_key]
    tallies = starts[1:] - starts[:-1]
    row_sorted = row_block[order]
    col_sorted = col_block[order]
    keep = (sorted_key < devices) & (rank_in < TILES_DEV)
    slot = jnp.where(keep, sorted_key * TILES_DEV + rank_in, slot_total)
    lists = jnp.zeros((3, slot_total), jnp.int32)
    lists = lists.at[0, slot].set(row_sorted % row_span, mode='drop')
    lists = lists.at[1, slot].set(col_sorted // row_span * BPD + col_sorted % BPD, mode='drop')
    lists = lists.at[2, slot].set(1, mode='drop')
    chosen = jax.random.randint(jax.random.fold_in(key, 31), (), 0, devices)
    chosen_row = chosen // N_COL
    chosen_col = chosen % N_COL
    taken = jnp.minimum(tallies[chosen], TILES_DEV)
    pool_row = jnp.arange(row_span, dtype=jnp.int32)[:, None]
    pool_col = jnp.arange(col_span, dtype=jnp.int32)[None, :]
    global_row = chosen_row * row_span + pool_row
    global_col = (pool_col // BPD * N_COL + chosen_col) * BPD + pool_col % BPD
    apart_x = jnp.abs(cell_x[global_row] - cell_x[global_col])
    apart_y = jnp.abs(cell_y[global_row] - cell_y[global_col])
    distant = (jnp.maximum(apart_x, apart_y) >= 2) & (global_row < global_col)
    ranking = jax.random.permutation(jax.random.fold_in(key, 41), row_span * col_span).astype(jnp.int32)
    score = jnp.where(distant.reshape(-1), ranking, -1)
    best_score, best_index = lax.top_k(score, TILES_DEV)
    extra_rank = jnp.arange(TILES_DEV, dtype=jnp.int32)
    extra_use = (extra_rank < TILES_DEV - taken) & (best_score >= 0)
    extra_slot = jnp.where(extra_use, chosen * TILES_DEV + taken + extra_rank, slot_total)
    lists = lists.at[0, extra_slot].set(best_index // col_span, mode='drop')
    lists = lists.at[1, extra_slot].set(best_index % col_span, mode='drop')
    lists = lists.at[2, extra_slot].set(1, mode='drop')
    return lists


def setup_inputs(seed: int = 0) -> dict:
    streams_of = jax.random.split(jax.random.key(seed), 4)
    return {
        "points": draw_points(jax.random.fold_in(streams_of[3], 71), 0),
        "values": draw_values(jax.random.fold_in(streams_of[3], 71), 0),
        "tile_lists": draw_tile_lists(jax.random.fold_in(streams_of[3], 71), 0),
    }


support = 0.5
ridge_shift = 1.0

def wendland(left, right):
    offsets = left[:, :, :, None] - right[:, :, None, :]
    distance = jnp.sqrt(lax.optimization_barrier(jnp.sum(offsets * offsets, axis=0)))
    scaled = distance / support
    remain = jnp.maximum(1.0 - scaled, 0.0)
    return remain * remain * remain * remain * (4.0 * scaled + 1.0)

def reference(points, values, tile_lists):
    slot_ids = jnp.arange(tile_lists.shape[1], dtype=jnp.int32)
    device = slot_ids // TILES_DEV
    row_id = device // N_COL
    col_id = device % N_COL
    row_block = row_id * (N_COL * BPD) + tile_lists[0]
    col_block = (tile_lists[1] // BPD * N_COL + col_id) * BPD + tile_lists[1] % BPD
    weight = tile_lists[2].astype(jnp.float32)
    mirror_weight = weight * (row_block != col_block).astype(jnp.float32)
    point_blocks = points.reshape(3, NBLK, BLK)
    group_shape = (N_ROW * N_COL, TILES_DEV)
    groups = (row_block.reshape(group_shape), col_block.reshape(group_shape), weight.reshape(group_shape), mirror_weight.reshape(group_shape))

    def operate(vector):
        blocks = vector.reshape(NRHS, NBLK, BLK)

        def visit_group(result_sum, member_set):
            row_index, col_index, row_weight, col_weight = member_set
            kernel = wendland(point_blocks[:, row_index], point_blocks[:, col_index])
            forward = jnp.einsum('gxy,fgy->fgx', kernel, blocks[:, col_index], precision=lax.Precision.HIGHEST)
            behind = jnp.einsum('gxy,fgx->fgy', kernel, blocks[:, row_index], precision=lax.Precision.HIGHEST)
            result_sum = result_sum.at[:, row_index].add(forward * row_weight[None, :, None])
            result_sum = result_sum.at[:, col_index].add(behind * col_weight[None, :, None])
            return (result_sum, None)
        result_sum, _ = lax.scan(visit_group, jnp.zeros((NRHS, NBLK, BLK), jnp.float32), groups)
        return ridge_shift * vector + result_sum.reshape(NRHS, NPTS)
    solution = jnp.zeros_like(values)
    residual = values
    direction = values
    norm_now = lax.optimization_barrier(jnp.sum(residual * residual, axis=1))
    for iteration in range(ITERS):
        applied = operate(direction)
        step_length = norm_now / lax.optimization_barrier(jnp.sum(direction * applied, axis=1))
        solution = solution + step_length[:, None] * direction
        residual = residual - step_length[:, None] * applied
        norm_next = lax.optimization_barrier(jnp.sum(residual * residual, axis=1))
        direction = residual + (norm_next / norm_now)[:, None] * direction
        norm_now = norm_next
    return (solution, residual)
```

```python
import functools
import itertools

import jax
import jax.numpy as jnp
from jax import lax
from jax.experimental import pallas as pl
from jax.experimental.pallas import tpu as pltpu
from jax.sharding import PartitionSpec as P

BLK = 256
LANES = 128
CHUNK = 256

support = 0.5
ridge_shift = 1.0

SHIFT, VV, VW, QQ, QW, WW, QS, CROSS, WX = range(9)
HALF = 64


def pack_kernel(per_device, place_ref, values_ref, points_ref, lists_ref, out_ref):
    row_base = place_ref[0]
    col_id = place_ref[1]
    col_count = place_ref[2]
    x_step = place_ref[3]
    for b in range(per_device):
        for half in range(2):
            out_ref[2 * b + half] = values_ref[8 * half : 8 * half + 8, b * BLK : (b + 1) * BLK]
    for axis in range(3):
        for b in range(per_device):
            out_ref[2 * per_device + axis, b : b + 1, :] = points_ref[axis : axis + 1, b * BLK : (b + 1) * BLK]
    shift = per_device.bit_length() - 1
    low = per_device - 1

    def code(row, col, b):
        device = row * col_count + (col & 1) * x_step + lax.shift_right_logical(col, 1)
        return device * per_device + b

    row_local = lists_ref[0:1, :]
    col_local = lists_ref[1:2, :]
    live = lists_ref[2:3, :] == 1
    row_code = code(row_base, lax.shift_right_logical(row_local, shift), row_local & low)
    col_code = code(lax.shift_right_logical(col_local, shift), jnp.full_like(col_local, col_id), col_local & low)
    row_code = jnp.where(live, row_code, -1).astype(jnp.float32)
    col_code = jnp.where(live, col_code, -1).astype(jnp.float32)
    tiles = row_local.shape[1]
    last = 2 * per_device + 3
    out_ref[last] = jnp.full((8, BLK), -1.0, jnp.float32)
    out_ref[last, 0:1, 0:tiles] = row_code
    out_ref[last, 0:1, HALF : HALF + tiles] = col_code
    out_ref[last, 1:2, 0:tiles] = col_code
    out_ref[last, 1:2, HALF : HALF + tiles] = row_code


def split(x):
    high = x.astype(jnp.bfloat16)
    low = (x - high.astype(jnp.float32)).astype(jnp.bfloat16)
    return high, low


def work_kernel(
    pieces, per_device, cap, me_ref, *refs
):
    piece_refs = refs[:pieces]
    w_ref, x_ref, moment_ref = refs[pieces : pieces + 3]
    cloud, total, second, cache, stage, plan, lists, sems, list_sem = refs[pieces + 3 :]
    devices = cloud.shape[0]
    blocks = devices * per_device
    base = 2 * per_device
    block_shift = per_device.bit_length() - 1
    low_mask = per_device - 1
    run = devices // pieces
    copies = [
        pltpu.make_async_copy(ref, cloud.at[pl.ds(p * run, run)], sems.at[p]) for p, ref in enumerate(piece_refs)
    ]
    for copy in copies:
        copy.start()
    for copy in copies:
        copy.wait()

    mine = me_ref[0] * per_device
    ids = lax.broadcasted_iota(jnp.int32, (blocks, 2 * LANES), 0)

    def one_hot(pair, line):
        codes = []
        for k in range(2):
            row = cloud[2 * pair + k, base + 3, line : line + 1, 0:LANES].astype(jnp.int32)
            codes.append(jnp.where(row >= 0, row ^ mine, -1))
        codes = jnp.concatenate(codes, axis=1)
        return jnp.where(ids == codes, 1.0, 0.0).astype(jnp.bfloat16)

    stage[...] = jnp.zeros_like(stage)

    def add_pairs(pair, carry):
        stage[...] += lax.dot_general(
            one_hot(pair, 0), one_hot(pair, 1), (((1,), (1,)), ((), ())), preferred_element_type=jnp.float32
        )
        return carry

    lax.fori_loop(0, devices // 2, add_pairs, 0)
    listed = stage[...] > 0.0
    rows = lax.broadcasted_iota(jnp.int32, (blocks, blocks), 0)
    cols = lax.broadcasted_iota(jnp.int32, (blocks, blocks), 1)
    near_row = jnp.max(stage[0:per_device, :], axis=0, keepdims=True) > 0.0
    near_row = near_row | (lax.broadcasted_iota(jnp.int32, (1, blocks), 1) < per_device)
    near_col = jnp.max(stage[:, 0:per_device], axis=1, keepdims=True) > 0.0
    near_col = near_col | (lax.broadcasted_iota(jnp.int32, (blocks, 1), 0) < per_device)
    near = jnp.where(near_row, 1.0, 0.0) + jnp.where(near_col, 1.0, 0.0)
    used = jnp.where(listed & (rows >= cols) & (near > 0.0), 1.0, 0.0)
    exact = dict(precision=lax.Precision.HIGHEST, preferred_element_type=jnp.float32)
    rank = jnp.dot(jnp.where(rows >= cols, 1.0, 0.0), used, **exact)
    count = jnp.broadcast_to(rank[blocks - 1 : blocks, :], (8, blocks))
    start = jnp.dot(count, jnp.where(rows < cols, 1.0, 0.0), **exact)
    whole = jnp.sum(count[0:1, :])
    own_count = jnp.sum(jnp.where(lax.broadcasted_iota(jnp.int32, (1, blocks), 1) < per_device, count[0:1, :], 0.0))
    n = whole.astype(jnp.int32)
    n_own = own_count.astype(jnp.int32)
    start_col = jnp.transpose(start)[:, 0:1]
    stop_col = start_col + jnp.transpose(count)[:, 0:1]
    stage[...] = rank * used
    index_col = lax.broadcasted_iota(jnp.int32, (blocks, CHUNK), 0).astype(jnp.float32)

    def write_list(chunk, carry):
        place = lax.broadcasted_iota(jnp.int32, (1, CHUNK), 1).astype(jnp.float32) + (chunk * CHUNK).astype(jnp.float32)
        pick = jnp.where((start_col <= place) & (place < stop_col), 1.0, 0.0)
        low_index = jnp.sum(pick * index_col, axis=0, keepdims=True)
        begin = jnp.sum(pick * start_col, axis=0, keepdims=True)
        ranks = jnp.dot(stage[...], pick, **exact)
        match = jnp.where(ranks == place - begin + 1.0, 1.0, 0.0)
        high_index = jnp.sum(match * index_col, axis=0, keepdims=True)
        both = jnp.concatenate([low_index, high_index, jnp.zeros((6, CHUNK), jnp.float32)], axis=0)
        plan[...] = both.astype(jnp.int32)
        copy = pltpu.make_async_copy(plan, lists.at[chunk], list_sem)
        copy.start()
        copy.wait()
        return carry

    lax.fori_loop(0, (n + CHUNK - 1) // CHUNK, write_list, 0)

    def entry(k):
        chunk = lax.shift_right_logical(k, CHUNK.bit_length() - 1)
        lane = k & (CHUNK - 1)
        return lists[chunk, 0, lane], lists[chunk, 1, lane]

    def point_rows(b):
        device = lax.shift_right_logical(b, block_shift)
        line = b & low_mask
        return [cloud[device, base + axis, pl.ds(line, 1), :] * (1.0 / support) for axis in range(3)]

    def evaluate(i, j, slot):
        across = point_rows(i)
        down = jnp.transpose(jnp.concatenate(point_rows(j) + [jnp.zeros((5, BLK), jnp.float32)], axis=0))
        for s in range(0, BLK, 32):
            square = None
            for axis in range(3):
                gap = down[s : s + 32, axis : axis + 1] - across[axis]
                square = gap * gap if square is None else square + gap * gap
            scaled = square * lax.rsqrt(jnp.maximum(square, 1e-30))
            remain = jnp.maximum(1.0 - scaled, 0.0)
            remain = remain * remain
            high, low = split(remain * remain * (4.0 * scaled + 1.0))
            cache[slot, 0, s : s + 32, :] = high
            cache[slot, 1, s : s + 32, :] = low

    def product(vector, slot, contract):
        high, low = split(vector)
        both = jnp.concatenate([high, low], axis=0)
        dims = (((1,), (contract,)), ((), ()))
        first = lax.dot_general(both, cache[slot, 0], dims, preferred_element_type=jnp.float32)
        second = lax.dot_general(high, cache[slot, 1], dims, preferred_element_type=jnp.float32)
        return first[0:16] + first[16:32] + second

    def values_of(b):
        device = lax.shift_right_logical(b, block_shift)
        return cloud[device, pl.ds(2 * (b & low_mask), 2)].reshape(16, BLK)

    for device in range(devices):
        total[device * per_device : (device + 1) * per_device] = cloud[device, 0:base].reshape(per_device, 16, BLK)

    def first_pass(k, carry):
        i, j = entry(k)
        slot = jnp.minimum(k, cap)
        evaluate(i, j, slot)
        total[i] += product(values_of(j), slot, 0)

        @pl.when(i != j)
        def _():
            total[j] += product(values_of(i), slot, 1)

        return carry

    lax.fori_loop(0, n, first_pass, 0)
    second[0:per_device] = total[0:per_device]

    def second_pass(k, carry):
        i, j = entry(k)
        slot = jnp.minimum(k, cap)

        @pl.when(k >= cap)
        def _():
            evaluate(i, j, slot)

        second[i] += product(total[j], slot, 0)

        @pl.when((i != j) & (j < per_device))
        def _():
            second[j] += product(total[i], slot, 1)

        return carry

    lax.fori_loop(0, n_own, second_pass, 0)
    w_ref[...] = total[0:per_device]
    x_ref[...] = second[0:per_device]

    v = cloud[0, 0:base].reshape(per_device, 16, BLK)
    w = total[0:per_device]
    x = second[0:per_device]

    def over(values):
        return jnp.sum(jnp.sum(values, axis=0), axis=1, keepdims=True)

    vv = over(v * v)
    vw = over(v * w)
    shift = jnp.where(vw != 0.0, vv / jnp.where(vw != 0.0, vw, 1.0), 0.0)
    q = v - shift[None] * w
    s = w - shift[None] * x
    sums = [shift, vv, vw, over(q * q), over(q * w), over(w * w), over(q * s), over(w * s + q * x), over(w * x)]
    lane = lax.broadcasted_iota(jnp.int32, (8, LANES), 1)
    sent = jnp.zeros((8, LANES), jnp.float32)
    for m, value in enumerate(sums):
        for half in range(2):
            sent = jnp.where(lane == half * HALF + m, value[8 * half : 8 * half + 8], sent)
    for device in range(devices):
        moment_ref[device] = sent


def finish_kernel(per_device, moment_ref, values_ref, w_ref, x_ref, solution_ref, residual_ref):
    moments = moment_ref[...]

    for half in range(2):

        def take(m):
            return moments[:, :, half * HALF + m : half * HALF + m + 1]

        def whole(values):
            return jnp.sum(values, axis=0)

        rr = whole(take(VV))
        vw = whole(take(VW))
        alpha = rr / vw
        delta = alpha[None] - take(SHIFT)
        fresh = whole(take(QQ) - 2.0 * delta * take(QW) + delta * delta * take(WW))
        mixed = whole(take(QW) - delta * take(WW))
        curve = whole(take(QS) - delta * take(CROSS) + delta * delta * take(WX))
        beta = fresh / rr
        curve = curve + 2.0 * beta * mixed + beta * beta * vw
        again = fresh / curve
        for b in range(per_device):
            at = (slice(8 * half, 8 * half + 8), slice(b * BLK, (b + 1) * BLK))
            v = values_ref[at]
            w = w_ref[b, 8 * half : 8 * half + 8, :]
            x = x_ref[b, 8 * half : 8 * half + 8, :]
            r = v - alpha * w
            d = r + beta * v
            solution_ref[at] = alpha * v + again * d
            residual_ref[at] = r - again * (w - alpha * x + beta * w)


def local(points, values, tile_lists):
    fields, owned_points = values.shape
    per_device = owned_points // BLK
    rows = lax.axis_size("row")
    cols = lax.axis_size("col")
    devices = rows * cols
    row_id = lax.axis_index("row")
    col_id = lax.axis_index("col")
    depth = cols // 2
    vmem = pl.BlockSpec(memory_space=pltpu.VMEM)
    smem = pl.BlockSpec(memory_space=pltpu.SMEM)
    anywhere = pl.BlockSpec(memory_space=pl.ANY)
    height = 2 * per_device + 4

    place = jnp.stack([row_id, col_id, jnp.int32(cols), jnp.int32(depth)]).astype(jnp.int32)
    packed = pl.pallas_call(
        functools.partial(pack_kernel, per_device),
        out_shape=jax.ShapeDtypeStruct((height, 8, BLK), jnp.float32),
        in_specs=[smem, vmem, vmem, vmem],
        out_specs=vmem,
        name="pack",
    )(place, values, points, tile_lists)

    def swap(array, row_mask, col_mask):
        if row_mask == 0:
            return lax.ppermute(array, "col", [(i, i ^ col_mask) for i in range(cols)])
        if col_mask == 0:
            return lax.ppermute(array, "row", [(i, i ^ row_mask) for i in range(rows)])
        pairs = [
            (r * cols + c, (r ^ row_mask) * cols + (c ^ col_mask)) for r in range(rows) for c in range(cols)
        ]
        return lax.ppermute(array, ("row", "col"), pairs)

    line = jnp.stack([packed] + [swap(packed, 0, 2 * z) for z in range(1, depth)])
    plane = {(0, 0): line}
    for row_mask, x in itertools.product(range(0, rows, 2), range(2)):
        if (row_mask, x) != (0, 0):
            plane[row_mask, x] = swap(line, row_mask, x)
    for (row_mask, x), part in list(plane.items()):
        plane[row_mask + 1, x] = swap(part, 1, 0)
    pieces = [plane[row_mask, x] for row_mask in range(rows) for x in range(2)]

    me = row_id * cols + (col_id & 1) * depth + lax.shift_right_logical(col_id, 1)
    blocks = devices * per_device
    chunks = (devices * tile_lists.shape[1] + CHUNK - 1) // CHUNK
    used = devices * height * 8 * BLK * 4 + blocks * 16 * BLK * 4 + blocks * blocks * 4
    cap = max(16, min(150, (56 * 2**20 - used - 6 * blocks * blocks * 4) // (BLK * BLK * 4)))
    block_shape = jax.ShapeDtypeStruct((per_device, fields, BLK), jnp.float32)
    w, x, moments = pl.pallas_call(
        functools.partial(work_kernel, len(pieces), per_device, cap),
        out_shape=(block_shape, block_shape, jax.ShapeDtypeStruct((devices, 8, LANES), jnp.float32)),
        in_specs=[smem] + [anywhere] * len(pieces),
        out_specs=(vmem, vmem, vmem),
        scratch_shapes=[
            pltpu.VMEM((devices, height, 8, BLK), jnp.float32),
            pltpu.VMEM((blocks, fields, BLK), jnp.float32),
            pltpu.VMEM((per_device, fields, BLK), jnp.float32),
            pltpu.VMEM((cap + 1, 2, BLK, BLK), jnp.bfloat16),
            pltpu.VMEM((blocks, blocks), jnp.float32),
            pltpu.VMEM((8, CHUNK), jnp.int32),
            pltpu.SMEM((chunks, 8, CHUNK), jnp.int32),
            pltpu.SemaphoreType.DMA((len(pieces),)),
            pltpu.SemaphoreType.DMA,
        ],
        compiler_params=pltpu.CompilerParams(vmem_limit_bytes=60 * 2**20),
        name="work",
    )(me.reshape(1).astype(jnp.int32), *pieces)
    moments = lax.all_to_all(moments, ("row", "col"), 0, 0, tiled=False)
    return pl.pallas_call(
        functools.partial(finish_kernel, per_device),
        out_shape=(jax.ShapeDtypeStruct(values.shape, jnp.float32),) * 2,
        in_specs=[vmem] * 4,
        out_specs=(vmem, vmem),
        name="finish",
    )(moments, values, w, x)


def solution(mesh):
    placed = (P(None, ("row", "col")), P(None, ("row", "col")), P(None, ("row", "col")))
    return jax.shard_map(
        local,
        mesh=mesh,
        in_specs=placed,
        out_specs=(P(None, ("row", "col")), P(None, ("row", "col"))),
        check_vma=False,
    )
```

```python
import functools
import itertools

import jax
import jax.numpy as jnp
from jax import lax
from jax.experimental import pallas as pl
from jax.experimental.pallas import tpu as pltpu
from jax.sharding import PartitionSpec as P

BLK = 256
LANES = 128
CHUNK = 256
GROUP = 8
UNROLL = 4

support = 0.5
ridge_shift = 1.0

SHIFT, VV, VW, QQ, QW, WW, QS, CROSS, WX = range(9)
HALF = 64


def pack_kernel(per_device, place_ref, values_ref, points_ref, lists_ref, blocks_ref, out_ref):
    row_base = place_ref[0]
    col_id = place_ref[1]
    col_count = place_ref[2]
    x_step = place_ref[3]
    for b in range(per_device):
        for half in range(2):
            blocks_ref[2 * b + half] = values_ref[8 * half : 8 * half + 8, b * BLK : (b + 1) * BLK]
    for axis in range(3):
        for b in range(per_device):
            out_ref[axis, b : b + 1, :] = points_ref[axis : axis + 1, b * BLK : (b + 1) * BLK] * (1.0 / support)
    shift = per_device.bit_length() - 1
    low = per_device - 1

    def code(row, col, b):
        device = row * col_count + (col & 1) * x_step + lax.shift_right_logical(col, 1)
        return device * per_device + b

    row_local = lists_ref[0:1, :]
    col_local = lists_ref[1:2, :]
    live = lists_ref[2:3, :] == 1
    row_code = code(row_base, lax.shift_right_logical(row_local, shift), row_local & low)
    col_code = code(lax.shift_right_logical(col_local, shift), jnp.full_like(col_local, col_id), col_local & low)
    row_code = jnp.where(live, row_code, -1).astype(jnp.float32)
    col_code = jnp.where(live, col_code, -1).astype(jnp.float32)
    tiles = row_local.shape[1]
    out_ref[3] = jnp.full((8, BLK), -1.0, jnp.float32)
    out_ref[3, 0:1, 0:tiles] = row_code
    out_ref[3, 0:1, HALF : HALF + tiles] = col_code
    out_ref[3, 1:2, 0:tiles] = col_code
    out_ref[3, 1:2, HALF : HALF + tiles] = row_code


def split(x):
    high = x.astype(jnp.bfloat16)
    low = (x - high.astype(jnp.float32)).astype(jnp.bfloat16)
    return high, low


def evaluate(across, down, high_ref, low_ref):
    down = jnp.transpose(jnp.concatenate(down + [jnp.zeros((5, BLK), jnp.float32)], axis=0))
    for s in range(0, BLK, 32):
        square = None
        for axis in range(3):
            gap = down[s : s + 32, axis : axis + 1] - across[axis]
            square = gap * gap if square is None else square + gap * gap
        scaled = square * lax.rsqrt(jnp.maximum(square, 1e-30))
        remain = jnp.maximum(1.0 - scaled, 0.0)
        remain = remain * remain
        high, low = split(remain * remain * (4.0 * scaled + 1.0))
        high_ref[s : s + 32, :] = high
        low_ref[s : s + 32, :] = low


def point_rows(cloud, b, per_device):
    device = lax.shift_right_logical(b, per_device.bit_length() - 1)
    line = b & (per_device - 1)
    return [cloud[device, axis, pl.ds(line, 1), :] for axis in range(3)]


def entry(lists, k):
    chunk = lax.shift_right_logical(k, CHUNK.bit_length() - 1)
    lane = k & (CHUNK - 1)
    return lists[chunk, 0, lane], lists[chunk, 1, lane]


def gather(refs, target, sems):
    run = target.shape[0] // len(refs)
    return [pltpu.make_async_copy(ref, target.at[pl.ds(p * run, run)], sems.at[p]) for p, ref in enumerate(refs)]


def tiles_kernel(pieces, per_device, cap, me_ref, *refs):
    list_ref, tile_ref = refs[pieces : pieces + 2]
    cloud, stage, plan, lists, ring, sems, list_sem, tile_sem = refs[pieces + 2 :]
    devices = cloud.shape[0]
    blocks = devices * per_device
    copies = gather(refs[:pieces], cloud, sems)
    for copy in copies:
        copy.start()
    for copy in copies:
        copy.wait()

    mine = me_ref[0] * per_device
    ids = lax.broadcasted_iota(jnp.int32, (blocks, 2 * LANES), 0)

    def one_hot(pair, line):
        codes = []
        for k in range(2):
            row = cloud[2 * pair + k, 3, line : line + 1, 0:LANES].astype(jnp.int32)
            codes.append(jnp.where(row >= 0, row ^ mine, -1))
        codes = jnp.concatenate(codes, axis=1)
        return jnp.where(ids == codes, 1.0, 0.0).astype(jnp.bfloat16)

    stage[...] = jnp.zeros_like(stage)

    def add_pairs(pair, carry):
        stage[...] += lax.dot_general(
            one_hot(pair, 0), one_hot(pair, 1), (((1,), (1,)), ((), ())), preferred_element_type=jnp.float32
        )
        return carry

    lax.fori_loop(0, devices // 2, add_pairs, 0)

    lane = lax.broadcasted_iota(jnp.int32, (blocks, LANES), 1)
    boxes = jnp.zeros((blocks, LANES), jnp.float32)
    for axis in range(3):
        coordinates = cloud[:, axis].reshape(blocks, BLK)
        boxes = jnp.where(lane == axis, jnp.min(coordinates, axis=1, keepdims=True), boxes)
        boxes = jnp.where(lane == 3 + axis, jnp.max(coordinates, axis=1, keepdims=True), boxes)
    flat = jnp.transpose(boxes)
    apart = None
    for axis in range(3):
        gap = jnp.maximum(
            boxes[:, axis : axis + 1] - flat[3 + axis : 4 + axis, :],
            flat[axis : axis + 1, :] - boxes[:, 3 + axis : 4 + axis],
        )
        gap = jnp.maximum(gap, 0.0)
        apart = gap * gap if apart is None else apart + gap * gap
    stage[...] = jnp.where(apart < 1.0001, stage[...], 0.0)

    listed = stage[...] > 0.0
    rows = lax.broadcasted_iota(jnp.int32, (blocks, blocks), 0)
    cols = lax.broadcasted_iota(jnp.int32, (blocks, blocks), 1)
    near_row = jnp.max(stage[0:per_device, :], axis=0, keepdims=True) > 0.0
    near_row = near_row | (lax.broadcasted_iota(jnp.int32, (1, blocks), 1) < per_device)
    near_col = jnp.max(stage[:, 0:per_device], axis=1, keepdims=True) > 0.0
    near_col = near_col | (lax.broadcasted_iota(jnp.int32, (blocks, 1), 0) < per_device)
    near = jnp.where(near_row, 1.0, 0.0) + jnp.where(near_col, 1.0, 0.0)
    used = jnp.where(listed & (rows >= cols) & (near > 0.0), 1.0, 0.0)
    exact = dict(precision=lax.Precision.HIGHEST, preferred_element_type=jnp.float32)
    rank = jnp.dot(jnp.where(rows >= cols, 1.0, 0.0), used, **exact)
    count = jnp.broadcast_to(rank[blocks - 1 : blocks, :], (8, blocks))
    start = jnp.dot(count, jnp.where(rows < cols, 1.0, 0.0), **exact)
    n = jnp.sum(count[0:1, :]).astype(jnp.int32)
    own = lax.broadcasted_iota(jnp.int32, (1, blocks), 1) < per_device
    n_own = jnp.sum(jnp.where(own, count[0:1, :], 0.0)).astype(jnp.int32)
    start_col = jnp.transpose(start)[:, 0:1]
    stop_col = start_col + jnp.transpose(count)[:, 0:1]
    stage[...] = rank * used
    index_col = lax.broadcasted_iota(jnp.int32, (blocks, CHUNK), 0).astype(jnp.float32)

    def write_list(chunk, carry):
        place = lax.broadcasted_iota(jnp.int32, (1, CHUNK), 1).astype(jnp.float32) + (chunk * CHUNK).astype(jnp.float32)
        pick = jnp.where((start_col <= place) & (place < stop_col), 1.0, 0.0)
        low_index = jnp.sum(pick * index_col, axis=0, keepdims=True)
        begin = jnp.sum(pick * start_col, axis=0, keepdims=True)
        ranks = jnp.dot(stage[...], pick, **exact)
        match = jnp.where(ranks == place - begin + 1.0, 1.0, 0.0)
        high_index = jnp.sum(match * index_col, axis=0, keepdims=True)
        both = jnp.concatenate([low_index, high_index], axis=0).astype(jnp.int32)
        sizes = jnp.concatenate(
            [jnp.full((1, CHUNK), n, jnp.int32), jnp.full((1, CHUNK), n_own, jnp.int32)], axis=0
        )
        plan[...] = jnp.concatenate([both, sizes, jnp.zeros((4, CHUNK), jnp.int32)], axis=0)
        list_ref[chunk] = plan[...]
        copy = pltpu.make_async_copy(plan, lists.at[chunk], list_sem)
        copy.start()
        copy.wait()
        return carry

    lax.fori_loop(0, jnp.maximum((n + CHUNK - 1) // CHUNK, 1), write_list, 0)

    def send(step):
        slot = step & 1
        return pltpu.make_async_copy(ring.at[slot], tile_ref.at[pl.ds(2 * step, 2)], tile_sem.at[slot])

    def write_tiles(step, carry):
        slot = step & 1

        @pl.when(step >= 2)
        def _():
            send(step - 2).wait()

        for part in range(2):
            i, j = entry(lists, 2 * step + part)
            evaluate(
                point_rows(cloud, i, per_device),
                point_rows(cloud, j, per_device),
                ring.at[slot, part, 0],
                ring.at[slot, part, 1],
            )
        send(step).start()
        return carry

    steps = (jnp.minimum(n, cap) + 1) // 2
    lax.fori_loop(0, steps, write_tiles, 0)
    for back in (2, 1):

        @pl.when(steps >= back)
        def _():
            send(steps - back).wait()


def apply_kernel(pieces, point_pieces, per_device, cap, lists, tile_ref, *refs):
    value_refs = refs[:pieces]
    point_refs = refs[pieces : pieces + point_pieces]
    w_ref, x_ref, moment_ref = refs[pieces + point_pieces : pieces + point_pieces + 3]
    field, total, second, cache, cloud, sems, total_sems, point_sems, tile_sems = refs[pieces + point_pieces + 3 :]
    devices = field.shape[0]
    blocks = devices * per_device
    block_shift = per_device.bit_length() - 1
    low_mask = per_device - 1
    n = lists[0, 2, 0]
    n_own = lists[0, 3, 0]
    held = jnp.minimum(n, cap)
    groups = (held + GROUP - 1) // GROUP

    def fetch(group):
        span = pl.ds(group * GROUP, GROUP)
        return pltpu.make_async_copy(tile_ref.at[span], cache.at[span], tile_sems.at[group])

    fills = gather(value_refs, field, sems) + gather(value_refs, total.at[pl.ds(0, devices)], total_sems)
    for copy in fills:
        copy.start()

    def start_fetch(group, carry):
        fetch(group).start()
        return carry

    lax.fori_loop(0, groups, start_fetch, 0)
    for copy in fills:
        copy.wait()

    def at(b):
        return lax.shift_right_logical(b, block_shift), pl.ds(2 * (b & low_mask), 2)

    def product(vector, slot, contract):
        high, low = split(vector)
        both = jnp.concatenate([high, low], axis=0)
        dims = (((1,), (contract,)), ((), ()))
        first = lax.dot_general(both, cache[slot, 0], dims, preferred_element_type=jnp.float32)
        later = lax.dot_general(high, cache[slot, 1], dims, preferred_element_type=jnp.float32)
        return (first[0:16] + first[16:32] + later).reshape(2, 8, BLK)

    def load(ref, b):
        device, span = at(b)
        return ref[device, span].reshape(16, BLK)

    def add(ref, b, value):
        device, span = at(b)
        ref[device, span] += value

    def evaluate_late(k):
        i, j = entry(lists, k)
        evaluate(
            point_rows(cloud, i, per_device), point_rows(cloud, j, per_device), cache.at[cap, 0], cache.at[cap, 1]
        )
        return i, j

    def first_group(group, carry):
        fetch(group).wait()
        for quad in range(0, GROUP, UNROLL):
            pending = []
            for u in range(UNROLL):
                k = group * GROUP + quad + u
                i, j = entry(lists, k)
                live = k < held
                pending.append((jnp.where(live, i, blocks), product(load(field, j), k, 0)))
                pending.append((jnp.where(live & (i != j), j, blocks), product(load(field, i), k, 1)))
            for b, value in pending:
                add(total, b, value)
        return carry

    lax.fori_loop(0, groups, first_group, 0)

    @pl.when(n > cap)
    def _():
        copies = gather(point_refs, cloud, point_sems)
        for copy in copies:
            copy.start()
        for copy in copies:
            copy.wait()

        def first_late(k, carry):
            i, j = evaluate_late(k)
            add(total, i, product(load(field, j), cap, 0))

            @pl.when(i != j)
            def _():
                add(total, j, product(load(field, i), cap, 1))

            return carry

        lax.fori_loop(cap, n, first_late, 0)

    second[0] = total[0]
    held_own = jnp.minimum(n_own, cap)

    def second_group(group, carry):
        pending = []
        for u in range(UNROLL):
            k = group * UNROLL + u
            i, j = entry(lists, k)
            live = k < held_own
            pending.append((jnp.where(live, i, per_device), product(load(total, j), k, 0)))
        for b, value in pending:
            add(second, b, value)
        for u in range(UNROLL):
            k = group * UNROLL + u
            i, j = entry(lists, k)

            @pl.when((k < held_own) & (i != j) & (j < per_device))
            def _():
                add(second, j, product(load(total, i), k, 1))

        return carry

    lax.fori_loop(0, (held_own + UNROLL - 1) // UNROLL, second_group, 0)

    def second_late(k, carry):
        i, j = evaluate_late(k)
        add(second, i, product(load(total, j), cap, 0))

        @pl.when((i != j) & (j < per_device))
        def _():
            add(second, j, product(load(total, i), cap, 1))

        return carry

    lax.fori_loop(cap, n_own, second_late, 0)

    v = field[0].reshape(per_device, 16, BLK)
    w = total[0].reshape(per_device, 16, BLK)
    x = second[0].reshape(per_device, 16, BLK)
    w_ref[...] = w
    x_ref[...] = x

    def over(values):
        return jnp.sum(jnp.sum(values, axis=0), axis=1, keepdims=True)

    vv = over(v * v)
    vw = over(v * w)
    shift = jnp.where(vw != 0.0, vv / jnp.where(vw != 0.0, vw, 1.0), 0.0)
    q = v - shift[None] * w
    s = w - shift[None] * x
    sums = [shift, vv, vw, over(q * q), over(q * w), over(w * w), over(q * s), over(w * s + q * x), over(w * x)]
    lane = lax.broadcasted_iota(jnp.int32, (8, LANES), 1)
    sent = jnp.zeros((8, LANES), jnp.float32)
    for m, value in enumerate(sums):
        for half in range(2):
            sent = jnp.where(lane == half * HALF + m, value[8 * half : 8 * half + 8], sent)
    for device in range(devices):
        moment_ref[device] = sent


def finish_kernel(per_device, moment_ref, values_ref, w_ref, x_ref, solution_ref, residual_ref):
    moments = moment_ref[...]

    for half in range(2):

        def take(m):
            return moments[:, :, half * HALF + m : half * HALF + m + 1]

        def whole(values):
            return jnp.sum(values, axis=0)

        rr = whole(take(VV))
        vw = whole(take(VW))
        alpha = rr / vw
        delta = alpha[None] - take(SHIFT)
        fresh = whole(take(QQ) - 2.0 * delta * take(QW) + delta * delta * take(WW))
        mixed = whole(take(QW) - delta * take(WW))
        curve = whole(take(QS) - delta * take(CROSS) + delta * delta * take(WX))
        beta = fresh / rr
        curve = curve + 2.0 * beta * mixed + beta * beta * vw
        again = fresh / curve
        for b in range(per_device):
            at = (slice(8 * half, 8 * half + 8), slice(b * BLK, (b + 1) * BLK))
            v = values_ref[at]
            w = w_ref[b, 8 * half : 8 * half + 8, :]
            x = x_ref[b, 8 * half : 8 * half + 8, :]
            r = v - alpha * w
            d = r + beta * v
            solution_ref[at] = alpha * v + again * d
            residual_ref[at] = r - again * (w - alpha * x + beta * w)


def local(points, values, tile_lists):
    fields, owned_points = values.shape
    per_device = owned_points // BLK
    rows = lax.axis_size("row")
    cols = lax.axis_size("col")
    devices = rows * cols
    row_id = lax.axis_index("row")
    col_id = lax.axis_index("col")
    depth = cols // 2
    vmem = pl.BlockSpec(memory_space=pltpu.VMEM)
    smem = pl.BlockSpec(memory_space=pltpu.SMEM)
    anywhere = pl.BlockSpec(memory_space=pl.ANY)
    height = 2 * per_device
    blocks = devices * per_device

    place = jnp.stack([row_id, col_id, jnp.int32(cols), jnp.int32(depth)]).astype(jnp.int32)
    own_values, own_points = pl.pallas_call(
        functools.partial(pack_kernel, per_device),
        out_shape=(
            jax.ShapeDtypeStruct((height, 8, BLK), jnp.float32),
            jax.ShapeDtypeStruct((4, per_device, BLK), jnp.float32),
        ),
        in_specs=[smem, vmem, vmem, vmem],
        out_specs=(vmem, vmem),
        name="pack",
    )(place, values, points, tile_lists)

    def swap(array, row_mask, col_mask):
        if row_mask == 0:
            return lax.ppermute(array, "col", [(i, i ^ col_mask) for i in range(cols)])
        if col_mask == 0:
            return lax.ppermute(array, "row", [(i, i ^ row_mask) for i in range(rows)])
        pairs = [
            (r * cols + c, (r ^ row_mask) * cols + (c ^ col_mask)) for r in range(rows) for c in range(cols)
        ]
        return lax.ppermute(array, ("row", "col"), pairs)

    def along(array):
        return jnp.stack([array] + [swap(array, 0, 2 * z) for z in range(1, depth)])

    def across(line):
        return {
            (row_mask, x): swap(line, row_mask, x) if (row_mask, x) != (0, 0) else line
            for row_mask, x in itertools.product(range(0, rows, 2), range(2))
        }

    def pairs(plane):
        plane = dict(plane)
        for (row_mask, x), part in list(plane.items()):
            plane[row_mask + 1, x] = swap(part, 1, 0)
        return [plane[row_mask, x] for row_mask in range(rows) for x in range(2)]

    point_parts = pairs(across(along(own_points)))
    value_line = along(own_values)
    value_line, point_parts = lax.optimization_barrier((value_line, point_parts))
    value_plane = across(value_line)

    me = row_id * cols + (col_id & 1) * depth + lax.shift_right_logical(col_id, 1)
    chunks = (devices * tile_lists.shape[1] + CHUNK - 1) // CHUNK
    used = 2 * blocks * fields * BLK * 4
    cap = max(GROUP, min(152, (54 * 2**20 - used) // (BLK * BLK * 4) // GROUP * GROUP))
    lists, tiles = pl.pallas_call(
        functools.partial(tiles_kernel, len(point_parts), per_device, cap),
        out_shape=(
            jax.ShapeDtypeStruct((chunks, 8, CHUNK), jnp.int32),
            jax.ShapeDtypeStruct((cap, 2, BLK, BLK), jnp.bfloat16),
        ),
        in_specs=[smem] + [anywhere] * len(point_parts),
        out_specs=(vmem, anywhere),
        scratch_shapes=[
            pltpu.VMEM((devices, 4, per_device, BLK), jnp.float32),
            pltpu.VMEM((blocks, blocks), jnp.float32),
            pltpu.VMEM((8, CHUNK), jnp.int32),
            pltpu.SMEM((chunks, 8, CHUNK), jnp.int32),
            pltpu.VMEM((2, 2, 2, BLK, BLK), jnp.bfloat16),
            pltpu.SemaphoreType.DMA((len(point_parts),)),
            pltpu.SemaphoreType.DMA,
            pltpu.SemaphoreType.DMA((2,)),
        ],
        compiler_params=pltpu.CompilerParams(vmem_limit_bytes=40 * 2**20),
        cost_estimate=pl.CostEstimate(flops=10**9, bytes_accessed=30 * 2**20, transcendentals=10**7),
        name="tiles",
    )(me.reshape(1).astype(jnp.int32), *point_parts)
    value_plane, lists, tiles = lax.optimization_barrier((value_plane, lists, tiles))
    value_parts = pairs(value_plane)
    block_shape = jax.ShapeDtypeStruct((per_device, fields, BLK), jnp.float32)
    w, x, moments = pl.pallas_call(
        functools.partial(apply_kernel, len(value_parts), len(point_parts), per_device, cap),
        out_shape=(block_shape, block_shape, jax.ShapeDtypeStruct((devices, 8, LANES), jnp.float32)),
        in_specs=[smem, anywhere] + [anywhere] * (len(value_parts) + len(point_parts)),
        out_specs=(vmem, vmem, vmem),
        scratch_shapes=[
            pltpu.VMEM((devices, height, 8, BLK), jnp.float32),
            pltpu.VMEM((devices + 1, height, 8, BLK), jnp.float32),
            pltpu.VMEM((2, height, 8, BLK), jnp.float32),
            pltpu.VMEM((cap + 1, 2, BLK, BLK), jnp.bfloat16),
            pltpu.VMEM((devices, 4, per_device, BLK), jnp.float32),
            pltpu.SemaphoreType.DMA((len(value_parts),)),
            pltpu.SemaphoreType.DMA((len(value_parts),)),
            pltpu.SemaphoreType.DMA((len(point_parts),)),
            pltpu.SemaphoreType.DMA((cap // GROUP,)),
        ],
        compiler_params=pltpu.CompilerParams(vmem_limit_bytes=60 * 2**20),
        name="apply",
    )(lists, tiles, *value_parts, *point_parts)
    moments = lax.all_to_all(moments, ("row", "col"), 0, 0, tiled=False)
    return pl.pallas_call(
        functools.partial(finish_kernel, per_device),
        out_shape=(jax.ShapeDtypeStruct(values.shape, jnp.float32),) * 2,
        in_specs=[vmem] * 4,
        out_specs=(vmem, vmem),
        name="finish",
    )(moments, values, w, x)


def solution(mesh):
    placed = (P(None, ("row", "col")), P(None, ("row", "col")), P(None, ("row", "col")))
    return jax.shard_map(
        local,
        mesh=mesh,
        in_specs=placed,
        out_specs=(P(None, ("row", "col")), P(None, ("row", "col"))),
        check_vma=False,
    )
```

```python
import functools
import itertools

import jax
import jax.numpy as jnp
from jax import lax
from jax.experimental import pallas as pl
from jax.experimental.pallas import tpu as pltpu
from jax.sharding import PartitionSpec as P

BLK = 256
LANES = 128
CHUNK = 256
GROUP = 8
UNROLL = 4

support = 0.5
ridge_shift = 1.0

SHIFT, VV, VW, QQ, QW, WW, QS, CROSS, WX = range(9)
HALF = 64


def pack_kernel(per_device, place_ref, values_ref, points_ref, lists_ref, blocks_ref, out_ref):
    row_base = place_ref[0]
    col_id = place_ref[1]
    col_count = place_ref[2]
    x_step = place_ref[3]
    for b in range(per_device):
        for half in range(2):
            blocks_ref[2 * b + half] = values_ref[8 * half : 8 * half + 8, b * BLK : (b + 1) * BLK]
    for axis in range(3):
        for b in range(per_device):
            out_ref[axis, b : b + 1, :] = points_ref[axis : axis + 1, b * BLK : (b + 1) * BLK] * (1.0 / support)
    shift = per_device.bit_length() - 1
    low = per_device - 1

    def code(row, col, b):
        device = row * col_count + (col & 1) * x_step + lax.shift_right_logical(col, 1)
        return device * per_device + b

    row_local = lists_ref[0:1, :]
    col_local = lists_ref[1:2, :]
    live = lists_ref[2:3, :] == 1
    row_code = code(row_base, lax.shift_right_logical(row_local, shift), row_local & low)
    col_code = code(lax.shift_right_logical(col_local, shift), jnp.full_like(col_local, col_id), col_local & low)
    row_code = jnp.where(live, row_code, -1).astype(jnp.float32)
    col_code = jnp.where(live, col_code, -1).astype(jnp.float32)
    tiles = row_local.shape[1]
    out_ref[3] = jnp.full((8, BLK), -1.0, jnp.float32)
    out_ref[3, 0:1, 0:tiles] = row_code
    out_ref[3, 0:1, HALF : HALF + tiles] = col_code
    out_ref[3, 1:2, 0:tiles] = col_code
    out_ref[3, 1:2, HALF : HALF + tiles] = row_code
    lane = lax.broadcasted_iota(jnp.int32, (per_device, LANES), 1)
    boxes = jnp.zeros((per_device, LANES), jnp.float32)
    for axis in range(3):
        line = out_ref[axis]
        boxes = jnp.where(lane == axis, jnp.min(line, axis=1, keepdims=True), boxes)
        boxes = jnp.where(lane == 3 + axis, jnp.max(line, axis=1, keepdims=True), boxes)
    out_ref[3, :, LANES : 2 * LANES] = boxes


def split(x):
    high = x.astype(jnp.bfloat16)
    low = (x - high.astype(jnp.float32)).astype(jnp.bfloat16)
    return high, low


def shape_function(square):
    square = jnp.maximum(square, 1e-30)
    scaled = square * lax.rsqrt(square)
    remain = jnp.maximum(1.0 - scaled, 0.0)
    remain = remain * remain
    return remain * remain * (scaled + 0.25)


def evaluate(across, down, out_ref):
    down = jnp.transpose(jnp.concatenate(down + [jnp.zeros((5, BLK), jnp.float32)], axis=0))
    for s in range(0, BLK, 32):
        square = None
        for axis in range(3):
            gap = down[s : s + 32, axis : axis + 1] - across[axis]
            square = gap * gap if square is None else square + gap * gap
        high, low = split(shape_function(square))
        out_ref[0, s : s + 32, :] = high
        out_ref[1, s : s + 32, :] = low


def thirds(x):
    first = x.astype(jnp.bfloat16).astype(jnp.float32)
    rest = x - first
    second = rest.astype(jnp.bfloat16).astype(jnp.float32)
    return first, second, rest - second


def evaluate_flat(across, down, out_ref):
    blank = [jnp.zeros((5, BLK), jnp.float32)]
    q = jnp.concatenate(down + blank, axis=0)
    origin = q[:, 0:1]
    q = q - origin
    p = jnp.concatenate(across + blank, axis=0) - origin
    line = lax.broadcasted_iota(jnp.int32, (8, BLK), 0)
    qq = jnp.sum(q * q, axis=0, keepdims=True)
    pp = jnp.sum(p * p, axis=0, keepdims=True)
    q = jnp.where(line == 3, qq, jnp.where(line == 4, 1.0, q))
    p = jnp.where(line == 3, 1.0, jnp.where(line == 4, pp, -2.0 * p))
    q1, q2, q3 = thirds(q)
    p1, p2, p3 = thirds(p)
    left = jnp.concatenate([q1, q1, q2, q1, q3, q2], axis=0).astype(jnp.bfloat16)
    right = jnp.concatenate([p1, p2, p1, p3, p1, p2], axis=0).astype(jnp.bfloat16)
    square = lax.dot_general(left, right, (((0,), (0,)), ((), ())), preferred_element_type=jnp.float32)
    for s in range(0, BLK, 32):
        high, low = split(shape_function(square[s : s + 32]))
        out_ref[0, s : s + 32, :] = high
        out_ref[1, s : s + 32, :] = low


def point_rows(cloud, b, per_device):
    device = lax.shift_right_logical(b, per_device.bit_length() - 1)
    line = b & (per_device - 1)
    return [cloud[device, axis, pl.ds(line, 1), :] for axis in range(3)]


def entry(lists, k):
    chunk = lax.shift_right_logical(k, CHUNK.bit_length() - 1)
    lane = k & (CHUNK - 1)
    return lists[chunk, 0, lane], lists[chunk, 1, lane]


def gather(refs, target, sems):
    run = target.shape[0] // len(refs)
    return [pltpu.make_async_copy(ref, target.at[pl.ds(p * run, run)], sems.at[p]) for p, ref in enumerate(refs)]


def tiles_kernel(pieces, per_device, cap, me_ref, *refs):
    list_ref, tile_ref = refs[pieces : pieces + 2]
    cloud, stage, plan, lists, sems, list_sem = refs[pieces + 2 :]
    devices = cloud.shape[0]
    blocks = devices * per_device
    copies = gather(refs[:pieces], cloud, sems)
    for copy in copies:
        copy.start()
    for copy in copies:
        copy.wait()

    mine = me_ref[0] * per_device
    ids = lax.broadcasted_iota(jnp.int32, (blocks, LANES), 0)
    batch = 8

    def one_hot(device, line):
        row = cloud[device, 3, line : line + 1, 0:LANES].astype(jnp.int32)
        row = jnp.where(row >= 0, row ^ mine, -1)
        return jnp.where(ids == row, 1.0, 0.0).astype(jnp.bfloat16)

    def pairs_of(group):
        sides = [
            jnp.concatenate([one_hot(group * batch + k, line) for k in range(batch)], axis=1) for line in range(2)
        ]
        return lax.dot_general(*sides, (((1,), (1,)), ((), ())), preferred_element_type=jnp.float32)

    stage[...] = pairs_of(0)

    def add_pairs(group, carry):
        stage[...] += pairs_of(group)
        return carry

    lax.fori_loop(1, devices // batch, add_pairs, 0)

    boxes = cloud[:, 3, :, LANES : 2 * LANES].reshape(blocks, LANES)
    flat = jnp.transpose(boxes)
    extent = jnp.max(flat[3:6, :] - flat[0:3, :])
    apart = None
    for axis in range(3):
        gap = jnp.maximum(
            boxes[:, axis : axis + 1] - flat[3 + axis : 4 + axis, :],
            flat[axis : axis + 1, :] - boxes[:, 3 + axis : 4 + axis],
        )
        gap = jnp.maximum(gap, 0.0)
        apart = gap * gap if apart is None else apart + gap * gap
    stage[...] = jnp.where(apart < 1.0001, stage[...], 0.0)

    listed = stage[...] > 0.0
    rows = lax.broadcasted_iota(jnp.int32, (blocks, blocks), 0)
    cols = lax.broadcasted_iota(jnp.int32, (blocks, blocks), 1)
    near_row = jnp.max(stage[0:per_device, :], axis=0, keepdims=True) > 0.0
    near_row = near_row | (lax.broadcasted_iota(jnp.int32, (1, blocks), 1) < per_device)
    near_col = jnp.max(stage[:, 0:per_device], axis=1, keepdims=True) > 0.0
    near_col = near_col | (lax.broadcasted_iota(jnp.int32, (blocks, 1), 0) < per_device)
    near = jnp.where(near_row, 1.0, 0.0) + jnp.where(near_col, 1.0, 0.0)
    used = jnp.where(listed & (rows >= cols) & (near > 0.0), 1.0, 0.0)

    def counted(left, right):
        return jnp.dot(left.astype(jnp.bfloat16), right.astype(jnp.bfloat16), preferred_element_type=jnp.float32)

    rank = counted(jnp.where(rows >= cols, 1.0, 0.0), used)
    count = jnp.broadcast_to(rank[blocks - 1 : blocks, :], (8, blocks))
    start = jnp.sum(counted(used, jnp.where(rows < cols, 1.0, 0.0)), axis=0, keepdims=True)
    start = jnp.broadcast_to(start, (8, blocks))
    n = jnp.sum(count[0:1, :]).astype(jnp.int32)
    own = lax.broadcasted_iota(jnp.int32, (1, blocks), 1) < per_device
    n_own = jnp.sum(jnp.where(own, count[0:1, :], 0.0)).astype(jnp.int32)
    start_col = jnp.transpose(start)[:, 0:1]
    stop_col = start_col + jnp.transpose(count)[:, 0:1]
    stage[...] = rank * used
    index_col = lax.broadcasted_iota(jnp.int32, (blocks, CHUNK), 0).astype(jnp.float32)

    def write_list(chunk, carry):
        place = lax.broadcasted_iota(jnp.int32, (1, CHUNK), 1).astype(jnp.float32) + (chunk * CHUNK).astype(jnp.float32)
        pick = jnp.where((start_col <= place) & (place < stop_col), 1.0, 0.0)
        low_index = jnp.sum(pick * index_col, axis=0, keepdims=True)
        begin = jnp.sum(pick * start_col, axis=0, keepdims=True)
        high, low = split(stage[...])
        ranks = counted(high, pick) + counted(low, pick)
        match = jnp.where(ranks == place - begin + 1.0, 1.0, 0.0)
        high_index = jnp.sum(match * index_col, axis=0, keepdims=True)
        both = jnp.concatenate([low_index, high_index], axis=0).astype(jnp.int32)
        sizes = jnp.concatenate(
            [jnp.full((1, CHUNK), n, jnp.int32), jnp.full((1, CHUNK), n_own, jnp.int32)], axis=0
        )
        plan[...] = jnp.concatenate([both, sizes, jnp.zeros((4, CHUNK), jnp.int32)], axis=0)
        list_ref[chunk] = plan[...]
        copy = pltpu.make_async_copy(plan, lists.at[chunk], list_sem)
        copy.start()
        copy.wait()
        return carry

    lax.fori_loop(0, jnp.maximum((n + CHUNK - 1) // CHUNK, 1), write_list, 0)

    held = jnp.minimum(n, cap)

    def write_tiles(form, step):
        def body(k, carry):
            for part in range(step):
                i, j = entry(lists, k * step + part)
                form(
                    point_rows(cloud, i, per_device), point_rows(cloud, j, per_device), tile_ref.at[k * step + part]
                )
            return carry

        lax.fori_loop(0, (held + step - 1) // step, body, 0)

    @pl.when(extent <= 1.5 / support)
    def _():
        write_tiles(evaluate_flat, UNROLL)

    @pl.when(extent > 1.5 / support)
    def _():
        write_tiles(evaluate, 2)


def apply_kernel(pieces, point_pieces, per_device, cap, lists, tile_ref, *refs):
    value_refs = refs[:pieces]
    point_refs = refs[pieces : pieces + point_pieces]
    w_ref, x_ref, moment_ref = refs[pieces + point_pieces : pieces + point_pieces + 3]
    field, total, second, late, cloud, sems, point_sems = refs[pieces + point_pieces + 3 :]
    devices = field.shape[0]
    blocks = devices * per_device
    block_shift = per_device.bit_length() - 1
    low_mask = per_device - 1
    n = lists[0, 2, 0]
    n_own = lists[0, 3, 0]
    held = jnp.minimum(n, cap)
    fills = gather(value_refs, field, sems)
    for copy in fills:
        copy.start()
    total[...] = jnp.zeros_like(total)
    for copy in fills:
        copy.wait()

    def at(b):
        return lax.shift_right_logical(b, block_shift), pl.ds(2 * (b & low_mask), 2)

    def product(vector, tile, contract):
        high, low = split(4.0 * vector)
        both = jnp.concatenate([high, low], axis=0)
        dims = (((1,), (contract,)), ((), ()))
        first = lax.dot_general(both, tile[0], dims, preferred_element_type=jnp.float32)
        later = lax.dot_general(high, tile[1], dims, preferred_element_type=jnp.float32)
        return (first[0:16] + first[16:32] + later).reshape(2, 8, BLK)

    def load(ref, b):
        device, span = at(b)
        return ref[device, span].reshape(16, BLK)

    def add(ref, b, value):
        device, span = at(b)
        ref[device, span] += value

    def evaluate_late(k):
        i, j = entry(lists, k)
        evaluate(point_rows(cloud, i, per_device), point_rows(cloud, j, per_device), late)
        return i, j

    def image(b):
        return load(total, b) + load(field, b)

    def first_group(group, carry):
        pending = []
        for u in range(GROUP):
            k = group * GROUP + u
            i, j = entry(lists, k)
            live = k < held
            pending.append((jnp.where(live, i, blocks), product(load(field, j), tile_ref.at[k], 0)))
            pending.append((jnp.where(live & (i != j), j, blocks), product(load(field, i), tile_ref.at[k], 1)))
        for b, value in pending:
            add(total, b, value)
        return carry

    lax.fori_loop(0, (held + GROUP - 1) // GROUP, first_group, 0)

    @pl.when(n > cap)
    def _():
        copies = gather(point_refs, cloud, point_sems)
        for copy in copies:
            copy.start()
        for copy in copies:
            copy.wait()

        def first_late(k, carry):
            i, j = evaluate_late(k)
            add(total, i, product(load(field, j), late, 0))

            @pl.when(i != j)
            def _():
                add(total, j, product(load(field, i), late, 1))

            return carry

        lax.fori_loop(cap, n, first_late, 0)

    second[0] = total[0] + field[0]
    held_own = jnp.minimum(n_own, cap)

    def second_group(group, carry):
        pending = []
        for u in range(GROUP):
            k = group * GROUP + u
            i, j = entry(lists, k)
            live = k < held_own
            pending.append((jnp.where(live, i, per_device), product(image(j), tile_ref.at[k], 0)))
        for b, value in pending:
            add(second, b, value)
        for u in range(GROUP):
            k = group * GROUP + u
            i, j = entry(lists, k)

            @pl.when((k < held_own) & (i != j) & (j < per_device))
            def _():
                add(second, j, product(image(i), tile_ref.at[k], 1))

        return carry

    lax.fori_loop(0, (held_own + GROUP - 1) // GROUP, second_group, 0)

    def second_late(k, carry):
        i, j = evaluate_late(k)
        add(second, i, product(image(j), late, 0))

        @pl.when((i != j) & (j < per_device))
        def _():
            add(second, j, product(image(i), late, 1))

        return carry

    lax.fori_loop(cap, n_own, second_late, 0)

    v = field[0].reshape(per_device, 16, BLK)
    w = (total[0] + field[0]).reshape(per_device, 16, BLK)
    x = second[0].reshape(per_device, 16, BLK)
    w_ref[...] = w
    x_ref[...] = x

    def over(values):
        return jnp.sum(jnp.sum(values, axis=0), axis=1, keepdims=True)

    vv = over(v * v)
    vw = over(v * w)
    shift = jnp.where(vw != 0.0, vv / jnp.where(vw != 0.0, vw, 1.0), 0.0)
    q = v - shift[None] * w
    s = w - shift[None] * x
    sums = [shift, vv, vw, over(q * q), over(q * w), over(w * w), over(q * s), over(w * s + q * x), over(w * x)]
    lane = lax.broadcasted_iota(jnp.int32, (8, LANES), 1)
    sent = jnp.zeros((8, LANES), jnp.float32)
    for m, value in enumerate(sums):
        for half in range(2):
            sent = jnp.where(lane == half * HALF + m, value[8 * half : 8 * half + 8], sent)
    for device in range(devices):
        moment_ref[device] = sent


def finish_kernel(per_device, moment_ref, values_ref, w_ref, x_ref, solution_ref, residual_ref):
    moments = moment_ref[...]

    for half in range(2):

        def take(m):
            return moments[:, :, half * HALF + m : half * HALF + m + 1]

        def whole(values):
            return jnp.sum(values, axis=0)

        rr = whole(take(VV))
        vw = whole(take(VW))
        alpha = rr / vw
        delta = alpha[None] - take(SHIFT)
        fresh = whole(take(QQ) - 2.0 * delta * take(QW) + delta * delta * take(WW))
        mixed = whole(take(QW) - delta * take(WW))
        curve = whole(take(QS) - delta * take(CROSS) + delta * delta * take(WX))
        beta = fresh / rr
        curve = curve + 2.0 * beta * mixed + beta * beta * vw
        again = fresh / curve
        for b in range(per_device):
            at = (slice(8 * half, 8 * half + 8), slice(b * BLK, (b + 1) * BLK))
            v = values_ref[at]
            w = w_ref[b, 8 * half : 8 * half + 8, :]
            x = x_ref[b, 8 * half : 8 * half + 8, :]
            r = v - alpha * w
            d = r + beta * v
            solution_ref[at] = alpha * v + again * d
            residual_ref[at] = r - again * (w - alpha * x + beta * w)


def local(points, values, tile_lists):
    fields, owned_points = values.shape
    per_device = owned_points // BLK
    rows = lax.axis_size("row")
    cols = lax.axis_size("col")
    devices = rows * cols
    row_id = lax.axis_index("row")
    col_id = lax.axis_index("col")
    depth = cols // 2
    vmem = pl.BlockSpec(memory_space=pltpu.VMEM)
    smem = pl.BlockSpec(memory_space=pltpu.SMEM)
    anywhere = pl.BlockSpec(memory_space=pl.ANY)
    height = 2 * per_device
    blocks = devices * per_device

    place = jnp.stack([row_id, col_id, jnp.int32(cols), jnp.int32(depth)]).astype(jnp.int32)
    own_values, own_points = pl.pallas_call(
        functools.partial(pack_kernel, per_device),
        out_shape=(
            jax.ShapeDtypeStruct((height, 8, BLK), jnp.float32),
            jax.ShapeDtypeStruct((4, per_device, BLK), jnp.float32),
        ),
        in_specs=[smem, vmem, vmem, vmem],
        out_specs=(vmem, vmem),
        name="pack",
    )(place, values, points, tile_lists)

    def swap(array, row_mask, col_mask):
        if row_mask == 0:
            return lax.ppermute(array, "col", [(i, i ^ col_mask) for i in range(cols)])
        if col_mask == 0:
            return lax.ppermute(array, "row", [(i, i ^ row_mask) for i in range(rows)])
        pairs = [
            (r * cols + c, (r ^ row_mask) * cols + (c ^ col_mask)) for r in range(rows) for c in range(cols)
        ]
        return lax.ppermute(array, ("row", "col"), pairs)

    def along(array):
        return jnp.stack([array] + [swap(array, 0, 2 * z) for z in range(1, depth)])

    def across(line):
        return {
            (row_mask, x): swap(line, row_mask, x) if (row_mask, x) != (0, 0) else line
            for row_mask, x in itertools.product(range(0, rows, 2), range(2))
        }

    def pairs(plane):
        plane = dict(plane)
        for (row_mask, x), part in list(plane.items()):
            plane[row_mask + 1, x] = swap(part, 1, 0)
        return [plane[row_mask, x] for row_mask in range(rows) for x in range(2)]

    point_plane = across(along(own_points))
    value_line, point_plane = lax.optimization_barrier((along(own_values), point_plane))
    point_parts = pairs(point_plane)
    value_plane = across(value_line)

    me = row_id * cols + (col_id & 1) * depth + lax.shift_right_logical(col_id, 1)
    chunks = (devices * tile_lists.shape[1] + CHUNK - 1) // CHUNK
    tile_bytes = 4 * BLK * BLK
    cloud_bytes = devices * 4 * per_device * BLK * 4
    tiles_limit = cloud_bytes + 6 * 4 * blocks * blocks + 12 * 2**20
    apply_limit = cloud_bytes + 2 * blocks * fields * BLK * 4 + 10 * 2**20
    cap = max(GROUP, min(152, (60 * 2**20 - max(tiles_limit, apply_limit)) // tile_bytes // GROUP * GROUP))
    lists, tiles = pl.pallas_call(
        functools.partial(tiles_kernel, len(point_parts), per_device, cap),
        out_shape=(
            jax.ShapeDtypeStruct((chunks, 8, CHUNK), jnp.int32),
            pltpu.VMEM((cap, 2, BLK, BLK), jnp.bfloat16),
        ),
        in_specs=[smem] + [anywhere] * len(point_parts),
        out_specs=(vmem, vmem),
        scratch_shapes=[
            pltpu.VMEM((devices, 4, per_device, BLK), jnp.float32),
            pltpu.VMEM((blocks, blocks), jnp.float32),
            pltpu.VMEM((8, CHUNK), jnp.int32),
            pltpu.SMEM((chunks, 8, CHUNK), jnp.int32),
            pltpu.SemaphoreType.DMA((len(point_parts),)),
            pltpu.SemaphoreType.DMA,
        ],
        compiler_params=pltpu.CompilerParams(vmem_limit_bytes=tiles_limit),
        cost_estimate=pl.CostEstimate(flops=10**9, bytes_accessed=30 * 2**20, transcendentals=10**7),
        name="tiles",
    )(me.reshape(1).astype(jnp.int32), *point_parts)
    value_plane, lists, tiles = lax.optimization_barrier((value_plane, lists, tiles))
    value_parts = pairs(value_plane)
    block_shape = jax.ShapeDtypeStruct((per_device, fields, BLK), jnp.float32)
    w, x, moments = pl.pallas_call(
        functools.partial(apply_kernel, len(value_parts), len(point_parts), per_device, cap),
        out_shape=(block_shape, block_shape, jax.ShapeDtypeStruct((devices, 8, LANES), jnp.float32)),
        in_specs=[smem, vmem] + [anywhere] * (len(value_parts) + len(point_parts)),
        out_specs=(vmem, vmem, vmem),
        scratch_shapes=[
            pltpu.VMEM((devices, height, 8, BLK), jnp.float32),
            pltpu.VMEM((devices + 1, height, 8, BLK), jnp.float32),
            pltpu.VMEM((2, height, 8, BLK), jnp.float32),
            pltpu.VMEM((2, BLK, BLK), jnp.bfloat16),
            pltpu.VMEM((devices, 4, per_device, BLK), jnp.float32),
            pltpu.SemaphoreType.DMA((len(value_parts),)),
            pltpu.SemaphoreType.DMA((len(point_parts),)),
        ],
        compiler_params=pltpu.CompilerParams(vmem_limit_bytes=apply_limit),
        name="apply",
    )(lists, pltpu.with_memory_space_constraint(tiles, pltpu.VMEM), *value_parts, *point_parts)
    moments = lax.all_to_all(moments, ("row", "col"), 0, 0, tiled=False)
    return pl.pallas_call(
        functools.partial(finish_kernel, per_device),
        out_shape=(jax.ShapeDtypeStruct(values.shape, jnp.float32),) * 2,
        in_specs=[vmem] * 4,
        out_specs=(vmem, vmem),
        name="finish",
    )(moments, values, w, x)


def solution(mesh):
    placed = (P(None, ("row", "col")), P(None, ("row", "col")), P(None, ("row", "col")))
    return jax.shard_map(
        local,
        mesh=mesh,
        in_specs=placed,
        out_specs=(P(None, ("row", "col")), P(None, ("row", "col"))),
        check_vma=False,
    )
```

```python
import functools
import itertools

import jax
import jax.numpy as jnp
from jax import lax
from jax.experimental import pallas as pl
from jax.experimental.pallas import tpu as pltpu
from jax.sharding import PartitionSpec as P

BLK = 256
LANES = 128
CHUNK = 256
GROUP = 8

support = 0.5
ridge_shift = 1.0

SHIFT, QQ, QW, WW, QS, CROSS, WX = range(7)
HALF = 64


def pack_kernel(per_device, values_ref, points_ref, lists_ref, blocks_ref, out_ref):
    row_base = lax.axis_index("row")
    col_id = lax.axis_index("col")
    col_count = lax.axis_size("col")
    x_step = col_count // 2
    for b in range(per_device):
        for half in range(2):
            blocks_ref[2 * b + half] = values_ref[8 * half : 8 * half + 8, b * BLK : (b + 1) * BLK]
    for axis in range(3):
        for b in range(per_device):
            out_ref[axis, b : b + 1, :] = points_ref[axis : axis + 1, b * BLK : (b + 1) * BLK] * (1.0 / support)
    shift = per_device.bit_length() - 1
    low = per_device - 1

    def code(row, col, b):
        device = row * col_count + (col & 1) * x_step + lax.shift_right_logical(col, 1)
        return device * per_device + b

    row_local = lists_ref[0:1, :]
    col_local = lists_ref[1:2, :]
    live = lists_ref[2:3, :] == 1
    row_code = code(row_base, lax.shift_right_logical(row_local, shift), row_local & low)
    col_code = code(lax.shift_right_logical(col_local, shift), jnp.full_like(col_local, col_id), col_local & low)
    row_code = jnp.where(live, row_code, -1).astype(jnp.float32)
    col_code = jnp.where(live, col_code, -1).astype(jnp.float32)
    tiles = row_local.shape[1]
    out_ref[3] = jnp.full((8, BLK), -1.0, jnp.float32)
    out_ref[3, 0:1, 0:tiles] = row_code
    out_ref[3, 0:1, HALF : HALF + tiles] = col_code
    out_ref[3, 1:2, 0:tiles] = col_code
    out_ref[3, 1:2, HALF : HALF + tiles] = row_code
    lane = lax.broadcasted_iota(jnp.int32, (per_device, LANES), 1)
    boxes = jnp.zeros((per_device, LANES), jnp.float32)
    for axis in range(3):
        line = out_ref[axis]
        boxes = jnp.where(lane == axis, jnp.min(line, axis=1, keepdims=True), boxes)
        boxes = jnp.where(lane == 3 + axis, jnp.max(line, axis=1, keepdims=True), boxes)
    out_ref[3, :, LANES : 2 * LANES] = boxes


def split(x):
    high = x.astype(jnp.bfloat16)
    low = (x - high.astype(jnp.float32)).astype(jnp.bfloat16)
    return high, low


def shape_function(square):
    square = jnp.maximum(square, 1e-30)
    scaled = square * lax.rsqrt(square)
    remain = jnp.maximum(1.0 - scaled, 0.0)
    remain = remain * remain
    return remain * remain * (scaled + 0.25)


def evaluate(across, down, out_ref):
    down = jnp.transpose(jnp.concatenate(down + [jnp.zeros((5, BLK), jnp.float32)], axis=0))
    for s in range(0, BLK, 32):
        square = None
        for axis in range(3):
            gap = down[s : s + 32, axis : axis + 1] - across[axis]
            square = gap * gap if square is None else square + gap * gap
        high, low = split(shape_function(square))
        out_ref[0, s : s + 32, :] = high
        out_ref[1, s : s + 32, :] = low


def thirds(x):
    first = x.astype(jnp.bfloat16).astype(jnp.float32)
    rest = x - first
    second = rest.astype(jnp.bfloat16).astype(jnp.float32)
    return first, second, rest - second


def evaluate_flat(across, down, out_ref):
    blank = [jnp.zeros((5, BLK), jnp.float32)]
    q = jnp.concatenate(down + blank, axis=0)
    origin = q[:, 0:1]
    q = q - origin
    p = jnp.concatenate(across + blank, axis=0) - origin
    line = lax.broadcasted_iota(jnp.int32, (8, BLK), 0)
    qq = jnp.sum(q * q, axis=0, keepdims=True)
    pp = jnp.sum(p * p, axis=0, keepdims=True)
    q = jnp.where(line == 3, qq, jnp.where(line == 4, 1.0, q))
    p = jnp.where(line == 3, 1.0, jnp.where(line == 4, pp, -2.0 * p))
    q1, q2, q3 = thirds(q)
    p1, p2, p3 = thirds(p)
    left = jnp.concatenate([q1, q1, q2, q1, q3, q2], axis=0).astype(jnp.bfloat16)
    right = jnp.concatenate([p1, p2, p1, p3, p1, p2], axis=0).astype(jnp.bfloat16)
    square = lax.dot_general(left, right, (((0,), (0,)), ((), ())), preferred_element_type=jnp.float32)
    for s in range(0, BLK, 32):
        high, low = split(shape_function(square[s : s + 32]))
        out_ref[0, s : s + 32, :] = high
        out_ref[1, s : s + 32, :] = low


def point_rows(cloud, b, per_device):
    device = lax.shift_right_logical(b, per_device.bit_length() - 1)
    line = b & (per_device - 1)
    return [cloud[device, axis, pl.ds(line, 1), :] for axis in range(3)]


def entry(lists, kind, k):
    chunk = lax.shift_right_logical(k, CHUNK.bit_length() - 1)
    chunk = kind * (lists.shape[0] // 2) + jnp.minimum(chunk, lists.shape[0] // 2 - 1)
    code = lists[chunk, 0, k & (CHUNK - 1)]
    return code & 0xFFFF, lax.shift_right_logical(code, 16)


def sizes(lists, cap):
    found = []
    base = 0
    for kind in range(2):
        n = lists[kind * (lists.shape[0] // 2), 1, 0]
        held = jnp.minimum(n, jnp.maximum(cap - base, 0))
        found.append((n, held, base))
        base = base + held
    return found, lists[0, 1, 1]


def gather(refs, target, sems):
    run = target.shape[0] // len(refs)
    return [pltpu.make_async_copy(ref, target.at[pl.ds(p * run, run)], sems.at[p]) for p, ref in enumerate(refs)]


def tiles_kernel(pieces, per_device, cap, *refs):
    list_ref, tile_ref = refs[pieces : pieces + 2]
    cloud, stage, plan, lists, sems, list_sems = refs[pieces + 2 :]
    devices = cloud.shape[0]
    blocks = devices * per_device
    copies = gather(refs[:pieces], cloud, sems)
    for copy in copies:
        copy.start()
    for copy in copies:
        copy.wait()

    cols = lax.axis_size("col")
    col_id = lax.axis_index("col")
    mine = lax.axis_index("row") * cols + (col_id & 1) * (cols // 2) + lax.shift_right_logical(col_id, 1)
    mine = mine * per_device
    ids = lax.broadcasted_iota(jnp.int32, (blocks, LANES), 0)
    batch = 8

    def one_hot(device, line):
        row = cloud[device, 3, line : line + 1, 0:LANES].astype(jnp.int32)
        row = jnp.where(row >= 0, row ^ mine, -1)
        return jnp.where(ids == row, 1.0, 0.0).astype(jnp.bfloat16)

    def pairs_of(group):
        sides = [
            jnp.concatenate([one_hot(group * batch + k, line) for k in range(batch)], axis=1) for line in range(2)
        ]
        return lax.dot_general(*sides, (((1,), (1,)), ((), ())), preferred_element_type=jnp.float32)

    stage[...] = pairs_of(0)

    def add_pairs(group, carry):
        stage[...] += pairs_of(group)
        return carry

    lax.fori_loop(1, devices // batch, add_pairs, 0)

    boxes = cloud[:, 3, :, LANES : 2 * LANES].reshape(blocks, LANES)
    flat = jnp.transpose(boxes)
    extent = jnp.max(flat[3:6, :] - flat[0:3, :])
    apart = None
    for axis in range(3):
        gap = jnp.maximum(
            boxes[:, axis : axis + 1] - flat[3 + axis : 4 + axis, :],
            flat[axis : axis + 1, :] - boxes[:, 3 + axis : 4 + axis],
        )
        gap = jnp.maximum(gap, 0.0)
        apart = gap * gap if apart is None else apart + gap * gap
    stage[...] = jnp.where(apart < 1.0001, stage[...], 0.0)

    listed = stage[...] > 0.0
    rows = lax.broadcasted_iota(jnp.int32, (blocks, blocks), 0)
    columns = lax.broadcasted_iota(jnp.int32, (blocks, blocks), 1)
    near_row = jnp.max(stage[0:per_device, :], axis=0, keepdims=True) > 0.0
    near_row = near_row | (lax.broadcasted_iota(jnp.int32, (1, blocks), 1) < per_device)
    near_col = jnp.max(stage[:, 0:per_device], axis=1, keepdims=True) > 0.0
    near_col = near_col | (lax.broadcasted_iota(jnp.int32, (blocks, 1), 0) < per_device)

    def counted(left, right):
        return jnp.dot(left.astype(jnp.bfloat16), right.astype(jnp.bfloat16), preferred_element_type=jnp.float32)

    low_ids = lax.broadcasted_iota(jnp.int32, (blocks, CHUNK), 0).astype(jnp.float32)
    lower = jnp.where(rows >= columns, 1.0, 0.0)
    upper = jnp.where(rows < columns, 1.0, 0.0)

    def write_list(kind, used):
        rank = counted(lower, used)
        count = rank[blocks - 1 : blocks, :]
        start = jnp.sum(counted(used, upper), axis=0, keepdims=True)
        both = jnp.concatenate([start, start + count, jnp.zeros((6, blocks), jnp.float32)], axis=0)
        both = jnp.transpose(both)
        start_col = both[:, 0:1]
        stop_col = both[:, 1:2]
        n = jnp.sum(count).astype(jnp.int32)
        own = lax.broadcasted_iota(jnp.int32, (1, blocks), 1) < per_device
        n_own = jnp.sum(jnp.where(own, count, 0.0)).astype(jnp.int32)
        stage[...] = rank * used
        lane = lax.broadcasted_iota(jnp.int32, (1, CHUNK), 1)
        totals = jnp.where(lane == 0, n, n_own)
        first = kind * (list_ref.shape[0] // 2)

        def write(chunk, carry):
            place = lane.astype(jnp.float32) + (chunk * CHUNK).astype(jnp.float32)
            pick = jnp.where((start_col <= place) & (place < stop_col), 1.0, 0.0)
            column = jnp.sum(pick * low_ids, axis=0, keepdims=True)
            begin = jnp.sum(pick * start_col, axis=0, keepdims=True)
            high, low = split(stage[...])
            ranks = counted(high, pick) + counted(low, pick)
            match = jnp.where(ranks == place - begin + 1.0, 1.0, 0.0)
            row = jnp.sum(match * low_ids, axis=0, keepdims=True)
            code = row.astype(jnp.int32) * 65536 + column.astype(jnp.int32)
            plan[...] = jnp.concatenate([code, totals], axis=0)
            copies = [
                pltpu.make_async_copy(plan, lists.at[first + chunk], list_sems.at[0]),
                pltpu.make_async_copy(plan, list_ref.at[first + chunk], list_sems.at[1]),
            ]
            for copy in copies:
                copy.start()
            for copy in copies:
                copy.wait()
            return carry

        lax.fori_loop(0, jnp.maximum((n + CHUNK - 1) // CHUNK, 1), write, 0)

    write_list(0, jnp.where(listed & (rows >= columns) & near_row & near_col, 1.0, 0.0))
    write_list(1, jnp.where(listed & near_row & jnp.logical_not(near_col), 1.0, 0.0))
    kinds, _ = sizes(lists, cap)

    first_held = kinds[0][1]
    held = first_held + kinds[1][1]

    def write_tiles(form):
        def body(group, carry):
            for part in range(GROUP):
                slot = group * GROUP + part
                kind = (slot >= first_held).astype(jnp.int32)
                i, j = entry(lists, kind, slot - kind * first_held)
                form(point_rows(cloud, i, per_device), point_rows(cloud, j, per_device), tile_ref.at[slot])
            return carry

        lax.fori_loop(0, (held + GROUP - 1) // GROUP, body, 0)

    @pl.when(extent <= 1.5 / support)
    def _():
        write_tiles(evaluate_flat)

    @pl.when(extent > 1.5 / support)
    def _():
        write_tiles(evaluate)


def apply_kernel(pieces, point_pieces, per_device, cap, lists, tile_ref, *refs):
    value_refs = refs[:pieces]
    point_refs = refs[pieces : pieces + point_pieces]
    w_ref, x_ref, moment_ref = refs[pieces + point_pieces : pieces + point_pieces + 3]
    field, total, second, late, cloud, sems, point_sems = refs[pieces + point_pieces + 3 :]
    devices = field.shape[0]
    blocks = devices * per_device
    block_shift = per_device.bit_length() - 1
    low_mask = per_device - 1
    kinds, n_own = sizes(lists, cap)
    fills = gather(value_refs, field, sems)
    for copy in fills:
        copy.start()
    total[...] = jnp.zeros_like(total)
    for copy in fills:
        copy.wait()

    def at(b):
        return lax.shift_right_logical(b, block_shift), pl.ds(2 * (b & low_mask), 2)

    def product(vector, tile, contract):
        high, low = split(4.0 * vector)
        both = jnp.concatenate([high, low], axis=0)
        dims = (((1,), (contract,)), ((), ()))
        first = lax.dot_general(both, tile[0], dims, preferred_element_type=jnp.float32)
        later = lax.dot_general(high, tile[1], dims, preferred_element_type=jnp.float32)
        return (first[0:16] + first[16:32] + later).reshape(2, 8, BLK)

    def load(ref, b):
        device, span = at(b)
        return ref[device, span].reshape(16, BLK)

    def add(ref, b, value):
        device, span = at(b)
        ref[device, span] += value

    def image(b):
        return load(total, b) + load(field, b)

    def run(kind, held, source, target, spare, back):
        base = kinds[kind][2]

        def body(group, carry):
            def forward(u):
                k = group * GROUP + u
                i, j = entry(lists, kind, k)
                return jnp.where(k < held, i, spare), product(source(j), tile_ref.at[base + k], 0)

            def reverse(u):
                k = group * GROUP + u
                i, j = entry(lists, kind, k)
                wanted = (k < held) & (i != j) & (j < spare)
                return jnp.where(wanted, j, spare), product(source(i), tile_ref.at[base + k], 1)

            if back == "always":
                pending = [form(u) for u in range(GROUP) for form in (forward, reverse)]
            else:
                pending = [forward(u) for u in range(GROUP)]
            for b, value in pending:
                add(target, b, value)
            if back == "some":
                for u in range(GROUP):
                    k = group * GROUP + u
                    i, j = entry(lists, kind, k)

                    @pl.when((k < held) & (i != j) & (j < spare))
                    def _():
                        add(target, j, product(source(i), tile_ref.at[base + k], 1))

            return carry

        lax.fori_loop(0, (held + GROUP - 1) // GROUP, body, 0)

    def run_late(kind, first, last, source, target, spare):
        def body(k, carry):
            i, j = entry(lists, kind, k)
            evaluate(point_rows(cloud, i, per_device), point_rows(cloud, j, per_device), late)
            add(target, i, product(source(j), late, 0))
            if kind == 0:

                @pl.when((i != j) & (j < spare))
                def _():
                    add(target, j, product(source(i), late, 1))

            return carry

        lax.fori_loop(first, last, body, 0)

    def own_field(b):
        return load(field, b)

    run(0, kinds[0][1], own_field, total, blocks, "always")
    run(1, kinds[1][1], own_field, total, blocks, "never")

    @pl.when((kinds[0][0] > kinds[0][1]) | (kinds[1][0] > kinds[1][1]))
    def _():
        copies = gather(point_refs, cloud, point_sems)
        for copy in copies:
            copy.start()
        for copy in copies:
            copy.wait()
        for kind, (n, held, _) in enumerate(kinds):
            run_late(kind, held, n, own_field, total, blocks)

    second[0] = total[0] + field[0]
    held_own = jnp.minimum(n_own, kinds[0][1])
    run(0, held_own, image, second, per_device, "some")
    run_late(0, held_own, n_own, image, second, per_device)

    v = field[0].reshape(per_device, 16, BLK)
    w = (total[0] + field[0]).reshape(per_device, 16, BLK)
    x = second[0].reshape(per_device, 16, BLK)
    w_ref[...] = w
    x_ref[...] = x

    def over(values):
        return jnp.sum(jnp.sum(values, axis=0), axis=1, keepdims=True)

    vv = over(v * v)
    vw = over(v * w)
    shift = jnp.where(vw != 0.0, vv / jnp.where(vw != 0.0, vw, 1.0), 0.0)
    q = v - shift[None] * w
    s = w - shift[None] * x
    sums = [shift, over(q * q), over(q * w), over(w * w), over(q * s), over(w * s + q * x), over(w * x)]
    lane = lax.broadcasted_iota(jnp.int32, (16, LANES), 1)
    sent = jnp.zeros((16, LANES), jnp.float32)
    for m, value in enumerate(sums):
        sent = jnp.where(lane == m, value, sent)
    sent = jnp.concatenate([sent, jnp.zeros((LANES - 16, LANES), jnp.float32)], axis=0)
    sent = jnp.transpose(sent)[0:8]
    for device in range(devices):
        moment_ref[device] = sent


def finish_kernel(per_device, moment_ref, values_ref, w_ref, x_ref, solution_ref, residual_ref):
    def take(m):
        return moment_ref[:, m, :]

    def whole(values):
        return jnp.sum(values, axis=0, keepdims=True)

    shift, qq, qw, ww = take(SHIFT), take(QQ), take(QW), take(WW)
    rr = whole(qq + 2.0 * shift * qw + shift * shift * ww)
    vw = whole(qw + shift * ww)
    alpha = rr / vw
    delta = alpha - shift
    fresh = whole(qq - 2.0 * delta * qw + delta * delta * ww)
    mixed = whole(qw - delta * ww)
    curve = whole(take(QS) - delta * take(CROSS) + delta * delta * take(WX))
    beta = fresh / rr
    curve = curve + 2.0 * beta * mixed + beta * beta * vw
    again = fresh / curve
    steps = jnp.transpose(jnp.concatenate([alpha, beta, again, jnp.zeros((5, LANES), jnp.float32)], axis=0))
    for half in range(2):
        lines = slice(8 * half, 8 * half + 8)
        alpha, beta, again = (steps[lines, m : m + 1] for m in range(3))
        for b in range(per_device):
            at = (lines, slice(b * BLK, (b + 1) * BLK))
            v = values_ref[at]
            w = w_ref[b, lines, :]
            x = x_ref[b, lines, :]
            r = v - alpha * w
            d = r + beta * v
            solution_ref[at] = alpha * v + again * d
            residual_ref[at] = r - again * (w - alpha * x + beta * w)


def local(points, values, tile_lists):
    fields, owned_points = values.shape
    per_device = owned_points // BLK
    rows = lax.axis_size("row")
    cols = lax.axis_size("col")
    devices = rows * cols
    depth = cols // 2
    vmem = pl.BlockSpec(memory_space=pltpu.VMEM)
    smem = pl.BlockSpec(memory_space=pltpu.SMEM)
    anywhere = pl.BlockSpec(memory_space=pl.ANY)
    height = 2 * per_device
    blocks = devices * per_device

    own_values, own_points = pl.pallas_call(
        functools.partial(pack_kernel, per_device),
        out_shape=(
            jax.ShapeDtypeStruct((height, 8, BLK), jnp.float32),
            jax.ShapeDtypeStruct((4, per_device, BLK), jnp.float32),
        ),
        in_specs=[vmem, vmem, vmem],
        out_specs=(vmem, vmem),
        name="pack",
    )(values, points, tile_lists)

    def swap(array, row_mask, col_mask):
        if row_mask == 0:
            return lax.ppermute(array, "col", [(i, i ^ col_mask) for i in range(cols)])
        if col_mask == 0:
            return lax.ppermute(array, "row", [(i, i ^ row_mask) for i in range(rows)])
        pairs = [
            (r * cols + c, (r ^ row_mask) * cols + (c ^ col_mask)) for r in range(rows) for c in range(cols)
        ]
        return lax.ppermute(array, ("row", "col"), pairs)

    def along(array):
        return jnp.stack([array] + [swap(array, 0, 2 * z) for z in range(1, depth)])

    def across(line):
        return {
            (row_mask, x): swap(line, row_mask, x) if (row_mask, x) != (0, 0) else line
            for row_mask, x in itertools.product(range(0, rows, 2), range(2))
        }

    def pairs(plane):
        plane = dict(plane)
        for (row_mask, x), part in list(plane.items()):
            plane[row_mask + 1, x] = swap(part, 1, 0)
        return [plane[row_mask, x] for row_mask in range(rows) for x in range(2)]

    point_plane = across(along(own_points))
    value_line, point_plane = lax.optimization_barrier((along(own_values), point_plane))
    point_parts = pairs(point_plane)
    value_plane = across(value_line)

    chunks = (devices * tile_lists.shape[1] + CHUNK - 1) // CHUNK
    tile_bytes = 4 * BLK * BLK
    cloud_bytes = devices * 4 * per_device * BLK * 4
    field_bytes = blocks * fields * BLK * 4
    tiles_limit = cloud_bytes + 6 * 4 * blocks * blocks + 10 * 2**20
    apply_limit = cloud_bytes + 2 * field_bytes + 6 * 2**20
    room = 60 * 2**20 - max(tiles_limit, apply_limit)
    cap = max(GROUP, min(120, room // tile_bytes // GROUP * GROUP))
    lists, tiles = pl.pallas_call(
        functools.partial(tiles_kernel, len(point_parts), per_device, cap),
        out_shape=(
            pltpu.HBM((2 * chunks, 2, CHUNK), jnp.int32),
            pltpu.VMEM((cap, 2, BLK, BLK), jnp.bfloat16),
        ),
        in_specs=[anywhere] * len(point_parts),
        out_specs=(anywhere, vmem),
        scratch_shapes=[
            pltpu.VMEM((devices, 4, per_device, BLK), jnp.float32),
            pltpu.VMEM((blocks, blocks), jnp.float32),
            pltpu.VMEM((2, CHUNK), jnp.int32),
            pltpu.SMEM((2 * chunks, 2, CHUNK), jnp.int32),
            pltpu.SemaphoreType.DMA((len(point_parts),)),
            pltpu.SemaphoreType.DMA((2,)),
        ],
        compiler_params=pltpu.CompilerParams(vmem_limit_bytes=tiles_limit),
        cost_estimate=pl.CostEstimate(flops=10**9, bytes_accessed=30 * 2**20, transcendentals=10**7),
        name="tiles",
    )(*point_parts)
    value_plane, lists, tiles = lax.optimization_barrier((value_plane, lists, tiles))
    value_parts = pairs(value_plane)
    block_shape = jax.ShapeDtypeStruct((per_device, fields, BLK), jnp.float32)
    w, x, moments = pl.pallas_call(
        functools.partial(apply_kernel, len(value_parts), len(point_parts), per_device, cap),
        out_shape=(block_shape, block_shape, jax.ShapeDtypeStruct((devices, 8, LANES), jnp.float32)),
        in_specs=[smem, vmem] + [anywhere] * (len(value_parts) + len(point_parts)),
        out_specs=(vmem, vmem, vmem),
        scratch_shapes=[
            pltpu.VMEM((devices, height, 8, BLK), jnp.float32),
            pltpu.VMEM((devices + 1, height, 8, BLK), jnp.float32),
            pltpu.VMEM((2, height, 8, BLK), jnp.float32),
            pltpu.VMEM((2, BLK, BLK), jnp.bfloat16),
            pltpu.VMEM((devices, 4, per_device, BLK), jnp.float32),
            pltpu.SemaphoreType.DMA((len(value_parts),)),
            pltpu.SemaphoreType.DMA((len(point_parts),)),
        ],
        compiler_params=pltpu.CompilerParams(vmem_limit_bytes=apply_limit),
        name="apply",
    )(lists, pltpu.with_memory_space_constraint(tiles, pltpu.VMEM), *value_parts, *point_parts)
    moments = lax.all_to_all(moments, ("row", "col"), 0, 0, tiled=False)
    return pl.pallas_call(
        functools.partial(finish_kernel, per_device),
        out_shape=(jax.ShapeDtypeStruct(values.shape, jnp.float32),) * 2,
        in_specs=[vmem] * 4,
        out_specs=(vmem, vmem),
        name="finish",
    )(moments, values, w, x)


def solution(mesh):
    placed = (P(None, ("row", "col")), P(None, ("row", "col")), P(None, ("row", "col")))
    return jax.shard_map(
        local,
        mesh=mesh,
        in_specs=placed,
        out_specs=(P(None, ("row", "col")), P(None, ("row", "col"))),
        check_vma=False,
    )
```

```python
import functools
import itertools

import jax
import jax.numpy as jnp
from jax import lax
from jax.experimental import pallas as pl
from jax.experimental.pallas import tpu as pltpu
from jax.sharding import PartitionSpec as P

BLK = 256
LANES = 128
CHUNK = 256
GROUP = 8

support = 0.5
ridge_shift = 1.0

SHIFT, QQ, QW, WW, QS, CROSS, WX = range(7)
HALF = 64


def pack_kernel(per_device, values_ref, points_ref, lists_ref, blocks_ref, out_ref):
    row_base = lax.axis_index("row")
    col_id = lax.axis_index("col")
    col_count = lax.axis_size("col")
    x_step = col_count // 2
    for b in range(per_device):
        for half in range(2):
            blocks_ref[2 * b + half] = values_ref[8 * half : 8 * half + 8, b * BLK : (b + 1) * BLK]
    for axis in range(3):
        for b in range(per_device):
            out_ref[axis, b : b + 1, :] = points_ref[axis : axis + 1, b * BLK : (b + 1) * BLK] * (1.0 / support)
    shift = per_device.bit_length() - 1
    low = per_device - 1

    def code(row, col, b):
        device = row * col_count + (col & 1) * x_step + lax.shift_right_logical(col, 1)
        return device * per_device + b

    row_local = lists_ref[0:1, :]
    col_local = lists_ref[1:2, :]
    live = lists_ref[2:3, :] == 1
    row_code = code(row_base, lax.shift_right_logical(row_local, shift), row_local & low)
    col_code = code(lax.shift_right_logical(col_local, shift), jnp.full_like(col_local, col_id), col_local & low)
    row_code = jnp.where(live, row_code, -1).astype(jnp.float32)
    col_code = jnp.where(live, col_code, -1).astype(jnp.float32)
    tiles = row_local.shape[1]
    out_ref[3] = jnp.full((8, BLK), -1.0, jnp.float32)
    out_ref[3, 0:1, 0:tiles] = row_code
    out_ref[3, 0:1, HALF : HALF + tiles] = col_code
    out_ref[3, 1:2, 0:tiles] = col_code
    out_ref[3, 1:2, HALF : HALF + tiles] = row_code
    lane = lax.broadcasted_iota(jnp.int32, (per_device, LANES), 1)
    boxes = jnp.zeros((per_device, LANES), jnp.float32)
    for axis in range(3):
        line = out_ref[axis]
        boxes = jnp.where(lane == axis, jnp.min(line, axis=1, keepdims=True), boxes)
        boxes = jnp.where(lane == 3 + axis, jnp.max(line, axis=1, keepdims=True), boxes)
    out_ref[3, :, LANES : 2 * LANES] = boxes


def split(x):
    high = x.astype(jnp.bfloat16)
    low = (x - high.astype(jnp.float32)).astype(jnp.bfloat16)
    return high, low


def shape_function(square):
    square = jnp.maximum(square, 1e-30)
    scaled = square * lax.rsqrt(square)
    remain = jnp.maximum(1.0 - scaled, 0.0)
    remain = remain * remain
    return remain * remain * (scaled + 0.25)


def evaluate(across, down, out_ref):
    down = jnp.transpose(jnp.concatenate(down + [jnp.zeros((5, BLK), jnp.float32)], axis=0))
    for s in range(0, BLK, 32):
        square = None
        for axis in range(3):
            gap = down[s : s + 32, axis : axis + 1] - across[axis]
            square = gap * gap if square is None else square + gap * gap
        high, low = split(shape_function(square))
        out_ref[0, s : s + 32, :] = high
        out_ref[1, s : s + 32, :] = low


def thirds(x):
    first = x.astype(jnp.bfloat16).astype(jnp.float32)
    rest = x - first
    second = rest.astype(jnp.bfloat16).astype(jnp.float32)
    return first, second, rest - second


def evaluate_flat(across, down, out_ref):
    blank = [jnp.zeros((5, BLK), jnp.float32)]
    q = jnp.concatenate(down + blank, axis=0)
    origin = q[:, 0:1]
    q = q - origin
    p = jnp.concatenate(across + blank, axis=0) - origin
    line = lax.broadcasted_iota(jnp.int32, (8, BLK), 0)
    qq = jnp.sum(q * q, axis=0, keepdims=True)
    pp = jnp.sum(p * p, axis=0, keepdims=True)
    q = jnp.where(line == 3, qq, jnp.where(line == 4, 1.0, q))
    p = jnp.where(line == 3, 1.0, jnp.where(line == 4, pp, -2.0 * p))
    q1, q2, q3 = thirds(q)
    p1, p2, p3 = thirds(p)
    left = jnp.concatenate([q1, q1, q2, q1, q3, q2], axis=0).astype(jnp.bfloat16)
    right = jnp.concatenate([p1, p2, p1, p3, p1, p2], axis=0).astype(jnp.bfloat16)
    square = lax.dot_general(left, right, (((0,), (0,)), ((), ())), preferred_element_type=jnp.float32)
    for s in range(0, BLK, 32):
        high, low = split(shape_function(square[s : s + 32]))
        out_ref[0, s : s + 32, :] = high
        out_ref[1, s : s + 32, :] = low


def point_rows(cloud, b, per_device):
    device = lax.shift_right_logical(b, per_device.bit_length() - 1)
    line = b & (per_device - 1)
    return [cloud[device, axis, pl.ds(line, 1), :] for axis in range(3)]


def entry(lists, kind, k):
    chunk = lax.shift_right_logical(k, CHUNK.bit_length() - 1)
    chunk = kind * (lists.shape[0] // 2) + jnp.minimum(chunk, lists.shape[0] // 2 - 1)
    code = lists[chunk, 0, k & (CHUNK - 1)]
    return code & 0xFFFF, lax.shift_right_logical(code, 16)


def sizes(lists, cap):
    found = []
    base = 0
    for kind in range(2):
        chunk = kind * (lists.shape[0] // 2)
        n = lists[chunk, 1, 0]
        held = jnp.minimum(n, jnp.maximum(cap - base, 0))
        found.append((n, lists[chunk, 1, 1], held, base))
        base = base + held
    return found


def gather(refs, target, sems):
    run = target.shape[0] // len(refs)
    return [pltpu.make_async_copy(ref, target.at[pl.ds(p * run, run)], sems.at[p]) for p, ref in enumerate(refs)]


def tiles_kernel(pieces, per_device, cap, *refs):
    list_ref, tile_ref = refs[pieces : pieces + 2]
    cloud, stage, plan, lists, sems, list_sems = refs[pieces + 2 :]
    devices = cloud.shape[0]
    blocks = devices * per_device
    copies = gather(refs[:pieces], cloud, sems)
    for copy in copies:
        copy.start()
    for copy in copies:
        copy.wait()

    cols = lax.axis_size("col")
    col_id = lax.axis_index("col")
    mine = lax.axis_index("row") * cols + (col_id & 1) * (cols // 2) + lax.shift_right_logical(col_id, 1)
    mine = mine * per_device
    ids = lax.broadcasted_iota(jnp.int32, (blocks, LANES), 0)
    batch = 8

    def one_hot(device, line):
        row = cloud[device, 3, line : line + 1, 0:LANES].astype(jnp.int32)
        row = jnp.where(row >= 0, row ^ mine, -1)
        return jnp.where(ids == row, 1.0, 0.0).astype(jnp.bfloat16)

    def pairs_of(group):
        sides = [
            jnp.concatenate([one_hot(group * batch + k, line) for k in range(batch)], axis=1) for line in range(2)
        ]
        return lax.dot_general(*sides, (((1,), (1,)), ((), ())), preferred_element_type=jnp.float32)

    stage[...] = pairs_of(0)

    def add_pairs(group, carry):
        stage[...] += pairs_of(group)
        return carry

    lax.fori_loop(1, devices // batch, add_pairs, 0)

    boxes = cloud[:, 3, :, LANES : 2 * LANES].reshape(blocks, LANES)
    flat = jnp.transpose(boxes)
    extent = jnp.max(flat[3:6, :] - flat[0:3, :])
    apart = None
    for axis in range(3):
        gap = jnp.maximum(
            boxes[:, axis : axis + 1] - flat[3 + axis : 4 + axis, :],
            flat[axis : axis + 1, :] - boxes[:, 3 + axis : 4 + axis],
        )
        gap = jnp.maximum(gap, 0.0)
        apart = gap * gap if apart is None else apart + gap * gap
    stage[...] = jnp.where(apart < 1.0001, stage[...], 0.0)

    listed = stage[...] > 0.0
    rows = lax.broadcasted_iota(jnp.int32, (blocks, blocks), 0)
    columns = lax.broadcasted_iota(jnp.int32, (blocks, blocks), 1)
    near_row = jnp.max(stage[0:per_device, :], axis=0, keepdims=True) > 0.0
    near_row = near_row | (lax.broadcasted_iota(jnp.int32, (1, blocks), 1) < per_device)
    near_col = jnp.max(stage[:, 0:per_device], axis=1, keepdims=True) > 0.0
    near_col = near_col | (lax.broadcasted_iota(jnp.int32, (blocks, 1), 0) < per_device)

    def counted(left, right):
        return jnp.dot(left.astype(jnp.bfloat16), right.astype(jnp.bfloat16), preferred_element_type=jnp.float32)

    low_ids = lax.broadcasted_iota(jnp.int32, (blocks, CHUNK), 0).astype(jnp.float32)
    lower = jnp.where(rows >= columns, 1.0, 0.0)
    upper = jnp.where(rows < columns, 1.0, 0.0)

    def write_list(kind, used):
        rank = counted(lower, used)
        count = rank[blocks - 1 : blocks, :]
        start = jnp.sum(counted(used, upper), axis=0, keepdims=True)
        both = jnp.concatenate([start, start + count, jnp.zeros((6, blocks), jnp.float32)], axis=0)
        both = jnp.transpose(both)
        start_col = both[:, 0:1]
        stop_col = both[:, 1:2]
        n = jnp.sum(count).astype(jnp.int32)
        own = lax.broadcasted_iota(jnp.int32, (1, blocks), 1) < per_device
        n_own = jnp.sum(jnp.where(own, count, 0.0)).astype(jnp.int32)
        stage[...] = rank * used
        lane = lax.broadcasted_iota(jnp.int32, (1, CHUNK), 1)
        totals = jnp.where(lane == 0, n, n_own)
        first = kind * (list_ref.shape[0] // 2)

        def write(chunk, place_in_plan):
            place = lane.astype(jnp.float32) + chunk * float(CHUNK)
            pick = jnp.where((start_col <= place) & (place < stop_col), 1.0, 0.0)
            column = jnp.sum(pick * low_ids, axis=0, keepdims=True)
            begin = jnp.sum(pick * start_col, axis=0, keepdims=True)
            high, low = split(stage[...])
            ranks = counted(high, pick) + counted(low, pick)
            match = jnp.where(ranks == place - begin + 1.0, 1.0, 0.0)
            row = jnp.sum(match * low_ids, axis=0, keepdims=True)
            code = row.astype(jnp.int32) * 65536 + column.astype(jnp.int32)
            plan[place_in_plan] = jnp.concatenate([code, totals], axis=0)

        def send(chunk, place_in_plan):
            return [
                pltpu.make_async_copy(plan.at[place_in_plan], target.at[first + chunk], list_sems.at[place_in_plan, k])
                for k, target in enumerate((lists, list_ref))
            ]

        def write_more(chunk, carry):
            write(chunk.astype(jnp.float32), 2)
            for copy in send(chunk, 2):
                copy.start()
            for copy in send(chunk, 2):
                copy.wait()
            return carry

        write(0.0, kind)
        for copy in send(0, kind):
            copy.start()
        lax.fori_loop(1, (n + CHUNK - 1) // CHUNK, write_more, 0)
        return send(0, kind)

    sent = [
        write_list(0, jnp.where(listed & (rows > columns) & near_row & near_col, 1.0, 0.0)),
        write_list(1, jnp.where(listed & near_row & ((rows == columns) | jnp.logical_not(near_col)), 1.0, 0.0)),
    ]
    for to_lists, _ in sent:
        to_lists.wait()
    kinds = sizes(lists, cap)

    first_held = kinds[0][2]
    held = first_held + kinds[1][2]

    def write_tiles(form):
        def body(group, carry):
            for part in range(GROUP):
                slot = group * GROUP + part
                kind = (slot >= first_held).astype(jnp.int32)
                i, j = entry(lists, kind, slot - kind * first_held)
                form(point_rows(cloud, i, per_device), point_rows(cloud, j, per_device), tile_ref.at[slot])
            return carry

        lax.fori_loop(0, (held + GROUP - 1) // GROUP, body, 0)

    @pl.when(extent <= 1.5 / support)
    def _():
        write_tiles(evaluate_flat)

    @pl.when(extent > 1.5 / support)
    def _():
        write_tiles(evaluate)

    for _, to_result in sent:
        to_result.wait()


def apply_kernel(pieces, point_pieces, per_device, cap, list_ref, tile_ref, *refs):
    value_refs = refs[:pieces]
    point_refs = refs[pieces : pieces + point_pieces]
    w_ref, x_ref, moment_ref = refs[pieces + point_pieces : pieces + point_pieces + 3]
    field, total, second, late, cloud, lists, sems, point_sems, list_sem = refs[pieces + point_pieces + 3 :]
    devices = field.shape[0]
    blocks = devices * per_device
    block_shift = per_device.bit_length() - 1
    low_mask = per_device - 1
    fills = [pltpu.make_async_copy(list_ref, lists, list_sem)] + gather(value_refs, field, sems)
    for copy in fills:
        copy.start()
    total[...] = jnp.zeros_like(total)
    for copy in fills:
        copy.wait()
    kinds = sizes(lists, cap)

    def at(b):
        return lax.shift_right_logical(b, block_shift), pl.ds(2 * (b & low_mask), 2)

    def product(vector, tile, contract):
        high, low = split(4.0 * vector)
        both = jnp.concatenate([high, low], axis=0)
        dims = (((1,), (contract,)), ((), ()))
        first = lax.dot_general(both, tile[0], dims, preferred_element_type=jnp.float32)
        later = lax.dot_general(high, tile[1], dims, preferred_element_type=jnp.float32)
        return (first[0:16] + first[16:32] + later).reshape(2, 8, BLK)

    def load(ref, b):
        device, span = at(b)
        return ref[device, span].reshape(16, BLK)

    def add(ref, b, value):
        device, span = at(b)
        ref[device, span] += value

    def image(b):
        return load(total, b) + load(field, b)

    def run(kind, held, source, target, spare, back):
        base = kinds[kind][3]

        def body(group, carry):
            pending = []
            for u in range(GROUP):
                k = group * GROUP + u
                i, j = entry(lists, kind, k)
                live = k < held
                pending.append((jnp.where(live, i, spare), product(source(j), tile_ref.at[base + k], 0)))
                if back == "always":
                    pending.append((jnp.where(live, j, spare), product(source(i), tile_ref.at[base + k], 1)))
            for b, value in pending:
                add(target, b, value)
            if back == "some":
                for u in range(GROUP):
                    k = group * GROUP + u
                    i, j = entry(lists, kind, k)

                    @pl.when((k < held) & (j < spare))
                    def _():
                        add(target, j, product(source(i), tile_ref.at[base + k], 1))

            return carry

        lax.fori_loop(0, (held + GROUP - 1) // GROUP, body, 0)

    def run_late(kind, first, last, source, target, spare):
        def body(k, carry):
            i, j = entry(lists, kind, k)
            evaluate(point_rows(cloud, i, per_device), point_rows(cloud, j, per_device), late)
            add(target, i, product(source(j), late, 0))
            if kind == 0:

                @pl.when(j < spare)
                def _():
                    add(target, j, product(source(i), late, 1))

            return carry

        lax.fori_loop(first, last, body, 0)

    def own_field(b):
        return load(field, b)

    run(0, kinds[0][2], own_field, total, blocks, "always")
    run(1, kinds[1][2], own_field, total, blocks, "never")

    @pl.when((kinds[0][0] > kinds[0][2]) | (kinds[1][0] > kinds[1][2]))
    def _():
        copies = gather(point_refs, cloud, point_sems)
        for copy in copies:
            copy.start()
        for copy in copies:
            copy.wait()
        for kind, (n, _, held, _) in enumerate(kinds):
            run_late(kind, held, n, own_field, total, blocks)

    second[0] = total[0] + field[0]
    for kind, back in enumerate(("some", "never")):
        _, n_own, held, _ = kinds[kind]
        held_own = jnp.minimum(n_own, held)
        run(kind, held_own, image, second, per_device, back)
        run_late(kind, held_own, n_own, image, second, per_device)

    v = field[0].reshape(per_device, 16, BLK)
    w = (total[0] + field[0]).reshape(per_device, 16, BLK)
    x = second[0].reshape(per_device, 16, BLK)
    w_ref[...] = w
    x_ref[...] = x

    def over(values):
        return jnp.sum(jnp.sum(values, axis=0), axis=1, keepdims=True)

    vv = over(v * v)
    vw = over(v * w)
    shift = jnp.where(vw != 0.0, vv / jnp.where(vw != 0.0, vw, 1.0), 0.0)
    q = v - shift[None] * w
    s = w - shift[None] * x
    sums = [shift, over(q * q), over(q * w), over(w * w), over(q * s), over(w * s + q * x), over(w * x)]
    lane = lax.broadcasted_iota(jnp.int32, (16, LANES), 1)
    sent = jnp.zeros((16, LANES), jnp.float32)
    for m, value in enumerate(sums):
        sent = jnp.where(lane == m, value, sent)
    sent = jnp.concatenate([sent, jnp.zeros((LANES - 16, LANES), jnp.float32)], axis=0)
    sent = jnp.transpose(sent)[0:8]
    for device in range(devices):
        moment_ref[device] = sent


def finish_kernel(per_device, moment_ref, values_ref, w_ref, x_ref, solution_ref, residual_ref):
    def take(m):
        return moment_ref[:, m, :]

    def whole(values):
        return jnp.sum(values, axis=0, keepdims=True)

    shift, qq, qw, ww = take(SHIFT), take(QQ), take(QW), take(WW)
    rr = whole(qq + 2.0 * shift * qw + shift * shift * ww)
    vw = whole(qw + shift * ww)
    alpha = rr / vw
    delta = alpha - shift
    fresh = whole(qq - 2.0 * delta * qw + delta * delta * ww)
    mixed = whole(qw - delta * ww)
    curve = whole(take(QS) - delta * take(CROSS) + delta * delta * take(WX))
    beta = fresh / rr
    curve = curve + 2.0 * beta * mixed + beta * beta * vw
    again = fresh / curve
    steps = jnp.transpose(jnp.concatenate([alpha, beta, again, jnp.zeros((5, LANES), jnp.float32)], axis=0))
    for half in range(2):
        lines = slice(8 * half, 8 * half + 8)
        alpha, beta, again = (steps[lines, m : m + 1] for m in range(3))
        for b in range(per_device):
            at = (lines, slice(b * BLK, (b + 1) * BLK))
            v = values_ref[at]
            w = w_ref[b, lines, :]
            x = x_ref[b, lines, :]
            r = v - alpha * w
            d = r + beta * v
            solution_ref[at] = alpha * v + again * d
            residual_ref[at] = r - again * (w - alpha * x + beta * w)


def local(points, values, tile_lists):
    fields, owned_points = values.shape
    per_device = owned_points // BLK
    rows = lax.axis_size("row")
    cols = lax.axis_size("col")
    devices = rows * cols
    depth = cols // 2
    vmem = pl.BlockSpec(memory_space=pltpu.VMEM)
    anywhere = pl.BlockSpec(memory_space=pl.ANY)
    height = 2 * per_device
    blocks = devices * per_device

    own_values, own_points = pl.pallas_call(
        functools.partial(pack_kernel, per_device),
        out_shape=(
            jax.ShapeDtypeStruct((height, 8, BLK), jnp.float32),
            jax.ShapeDtypeStruct((4, per_device, BLK), jnp.float32),
        ),
        in_specs=[vmem, vmem, vmem],
        out_specs=(vmem, vmem),
        name="pack",
    )(values, points, tile_lists)

    def swap(array, row_mask, col_mask):
        if row_mask == 0:
            return lax.ppermute(array, "col", [(i, i ^ col_mask) for i in range(cols)])
        if col_mask == 0:
            return lax.ppermute(array, "row", [(i, i ^ row_mask) for i in range(rows)])
        pairs = [
            (r * cols + c, (r ^ row_mask) * cols + (c ^ col_mask)) for r in range(rows) for c in range(cols)
        ]
        return lax.ppermute(array, ("row", "col"), pairs)

    def along(array):
        return jnp.stack([array] + [swap(array, 0, 2 * z) for z in range(1, depth)])

    def across(line):
        return {
            (row_mask, x): swap(line, row_mask, x) if (row_mask, x) != (0, 0) else line
            for row_mask, x in itertools.product(range(0, rows, 2), range(2))
        }

    def pairs(plane):
        plane = dict(plane)
        for (row_mask, x), part in list(plane.items()):
            plane[row_mask + 1, x] = swap(part, 1, 0)
        return [plane[row_mask, x] for row_mask in range(rows) for x in range(2)]

    point_plane = across(along(own_points))
    value_line, point_plane = lax.optimization_barrier((along(own_values), point_plane))
    point_parts = pairs(point_plane)
    value_plane = across(value_line)
    core_line = swap(value_line, 1, 0)

    chunks = (devices * tile_lists.shape[1] + CHUNK - 1) // CHUNK
    tile_bytes = 4 * BLK * BLK
    cloud_bytes = devices * 4 * per_device * BLK * 4
    field_bytes = blocks * fields * BLK * 4
    tiles_limit = cloud_bytes + 6 * 4 * blocks * blocks + 10 * 2**20
    apply_limit = cloud_bytes + 2 * field_bytes + 6 * 2**20
    room = 60 * 2**20 - max(tiles_limit, apply_limit)
    cap = max(GROUP, min(120, room // tile_bytes // GROUP * GROUP))
    lists, tiles = pl.pallas_call(
        functools.partial(tiles_kernel, len(point_parts), per_device, cap),
        out_shape=(
            pltpu.HBM((2 * chunks, 2, CHUNK), jnp.int32),
            pltpu.VMEM((cap, 2, BLK, BLK), jnp.bfloat16),
        ),
        in_specs=[anywhere] * len(point_parts),
        out_specs=(anywhere, vmem),
        scratch_shapes=[
            pltpu.VMEM((devices, 4, per_device, BLK), jnp.float32),
            pltpu.VMEM((blocks, blocks), jnp.float32),
            pltpu.VMEM((3, 2, CHUNK), jnp.int32),
            pltpu.SMEM((2 * chunks, 2, CHUNK), jnp.int32),
            pltpu.SemaphoreType.DMA((len(point_parts),)),
            pltpu.SemaphoreType.DMA((3, 2)),
        ],
        compiler_params=pltpu.CompilerParams(vmem_limit_bytes=tiles_limit),
        cost_estimate=pl.CostEstimate(flops=10**9, bytes_accessed=30 * 2**20, transcendentals=10**7),
        name="tiles",
    )(*point_parts)
    value_plane.pop((0, 0))
    value_plane, lists, tiles = lax.optimization_barrier((value_plane, lists, tiles))
    value_parts = [value_line, None, core_line, None] + [None] * (2 * rows - 4)
    for (row_mask, x), part in value_plane.items():
        value_parts[2 * row_mask + x] = part
        value_parts[2 * row_mask + 2 + x] = swap(part, 1, 0)
    block_shape = jax.ShapeDtypeStruct((per_device, fields, BLK), jnp.float32)
    w, x, moments = pl.pallas_call(
        functools.partial(apply_kernel, len(value_parts), len(point_parts), per_device, cap),
        out_shape=(block_shape, block_shape, jax.ShapeDtypeStruct((devices, 8, LANES), jnp.float32)),
        in_specs=[anywhere, vmem] + [anywhere] * (len(value_parts) + len(point_parts)),
        out_specs=(vmem, vmem, vmem),
        scratch_shapes=[
            pltpu.VMEM((devices, height, 8, BLK), jnp.float32),
            pltpu.VMEM((devices + 1, height, 8, BLK), jnp.float32),
            pltpu.VMEM((2, height, 8, BLK), jnp.float32),
            pltpu.VMEM((2, BLK, BLK), jnp.bfloat16),
            pltpu.VMEM((devices, 4, per_device, BLK), jnp.float32),
            pltpu.SMEM((2 * chunks, 2, CHUNK), jnp.int32),
            pltpu.SemaphoreType.DMA((len(value_parts),)),
            pltpu.SemaphoreType.DMA((len(point_parts),)),
            pltpu.SemaphoreType.DMA,
        ],
        compiler_params=pltpu.CompilerParams(vmem_limit_bytes=apply_limit),
        name="apply",
    )(
        pltpu.with_memory_space_constraint(lists, pltpu.HBM),
        pltpu.with_memory_space_constraint(tiles, pltpu.VMEM),
        *value_parts,
        *point_parts,
    )
    moments = lax.all_to_all(moments, ("row", "col"), 0, 0, tiled=False)
    return pl.pallas_call(
        functools.partial(finish_kernel, per_device),
        out_shape=(jax.ShapeDtypeStruct(values.shape, jnp.float32),) * 2,
        in_specs=[vmem] * 4,
        out_specs=(vmem, vmem),
        name="finish",
    )(moments, values, w, x)


def solution(mesh):
    placed = (P(None, ("row", "col")), P(None, ("row", "col")), P(None, ("row", "col")))
    return jax.shard_map(
        local,
        mesh=mesh,
        in_specs=placed,
        out_specs=(P(None, ("row", "col")), P(None, ("row", "col"))),
        check_vma=False,
    )
```

```python
import functools
import itertools

import jax
import jax.numpy as jnp
from jax import lax
from jax.experimental import pallas as pl
from jax.experimental.pallas import tpu as pltpu
from jax.sharding import PartitionSpec as P

BLK = 256
LANES = 128
CHUNK = 256
GROUP = 8
BATCH = 12

support = 0.5
ridge_shift = 1.0

SHIFT, QQ, QW, WW, QS, CROSS, WX = range(7)
HALF = 64


def pack_kernel(per_device, values_ref, points_ref, lists_ref, blocks_ref, out_ref):
    row_base = lax.axis_index("row")
    col_id = lax.axis_index("col")
    col_count = lax.axis_size("col")
    x_step = col_count // 2
    for b in range(per_device):
        for half in range(2):
            blocks_ref[2 * b + half] = values_ref[8 * half : 8 * half + 8, b * BLK : (b + 1) * BLK]
    for axis in range(3):
        for b in range(per_device):
            out_ref[axis, b : b + 1, :] = points_ref[axis : axis + 1, b * BLK : (b + 1) * BLK] * (1.0 / support)
    shift = per_device.bit_length() - 1
    low = per_device - 1

    def code(row, col, b):
        device = row * col_count + (col & 1) * x_step + lax.shift_right_logical(col, 1)
        return device * per_device + b

    row_local = lists_ref[0:1, :]
    col_local = lists_ref[1:2, :]
    live = lists_ref[2:3, :] == 1
    row_code = code(row_base, lax.shift_right_logical(row_local, shift), row_local & low)
    col_code = code(lax.shift_right_logical(col_local, shift), jnp.full_like(col_local, col_id), col_local & low)
    row_code = jnp.where(live, row_code, -1).astype(jnp.float32)
    col_code = jnp.where(live, col_code, -1).astype(jnp.float32)
    tiles = row_local.shape[1]
    out_ref[3] = jnp.full((8, BLK), -1.0, jnp.float32)
    out_ref[3, 0:1, 0:tiles] = row_code
    out_ref[3, 0:1, HALF : HALF + tiles] = col_code
    out_ref[3, 1:2, 0:tiles] = col_code
    out_ref[3, 1:2, HALF : HALF + tiles] = row_code
    lane = lax.broadcasted_iota(jnp.int32, (per_device, LANES), 1)
    boxes = jnp.zeros((per_device, LANES), jnp.float32)
    for axis in range(3):
        line = out_ref[axis]
        boxes = jnp.where(lane == axis, jnp.min(line, axis=1, keepdims=True), boxes)
        boxes = jnp.where(lane == 3 + axis, jnp.max(line, axis=1, keepdims=True), boxes)
    out_ref[3, :, LANES : 2 * LANES] = boxes


def split(x):
    high = x.astype(jnp.bfloat16)
    low = (x - high.astype(jnp.float32)).astype(jnp.bfloat16)
    return high, low


def shape_function(square):
    square = jnp.maximum(square, 1e-30)
    scaled = square * lax.rsqrt(square)
    remain = jnp.maximum(1.0 - scaled, 0.0)
    remain = remain * remain
    return remain * remain * (scaled + 0.25)


def evaluate(across, down, out_ref):
    down = jnp.transpose(jnp.concatenate(down + [jnp.zeros((5, BLK), jnp.float32)], axis=0))
    for s in range(0, BLK, 32):
        square = None
        for axis in range(3):
            gap = down[s : s + 32, axis : axis + 1] - across[axis]
            square = gap * gap if square is None else square + gap * gap
        high, low = split(shape_function(square))
        out_ref[0, s : s + 32, :] = high
        out_ref[1, s : s + 32, :] = low


def thirds(x):
    first = x.astype(jnp.bfloat16).astype(jnp.float32)
    rest = x - first
    second = rest.astype(jnp.bfloat16).astype(jnp.float32)
    return first, second, rest - second


def evaluate_flat(across, down, out_ref):
    blank = [jnp.zeros((5, BLK), jnp.float32)]
    q = jnp.concatenate(down + blank, axis=0)
    origin = q[:, 0:1]
    q = q - origin
    p = jnp.concatenate(across + blank, axis=0) - origin
    line = lax.broadcasted_iota(jnp.int32, (8, BLK), 0)
    qq = jnp.sum(q * q, axis=0, keepdims=True)
    pp = jnp.sum(p * p, axis=0, keepdims=True)
    q = jnp.where(line == 3, qq, jnp.where(line == 4, 1.0, q))
    p = jnp.where(line == 3, 1.0, jnp.where(line == 4, pp, -2.0 * p))
    q1, q2, q3 = thirds(q)
    p1, p2, p3 = thirds(p)
    left = jnp.concatenate([q1, q1, q2, q1, q3, q2], axis=0).astype(jnp.bfloat16)
    right = jnp.concatenate([p1, p2, p1, p3, p1, p2], axis=0).astype(jnp.bfloat16)
    square = lax.dot_general(left, right, (((0,), (0,)), ((), ())), preferred_element_type=jnp.float32)
    for s in range(0, BLK, 32):
        high, low = split(shape_function(square[s : s + 32]))
        out_ref[0, s : s + 32, :] = high
        out_ref[1, s : s + 32, :] = low


def point_rows(cloud, b, per_device):
    device = lax.shift_right_logical(b, per_device.bit_length() - 1)
    line = b & (per_device - 1)
    return [cloud[device, axis, pl.ds(line, 1), :] for axis in range(3)]


def entry(lists, kind, k):
    chunk = lax.shift_right_logical(k, CHUNK.bit_length() - 1)
    chunk = kind * (lists.shape[0] // 2) + jnp.minimum(chunk, lists.shape[0] // 2 - 1)
    code = lists[chunk, 0, k & (CHUNK - 1)]
    return code & 0xFFFF, lax.shift_right_logical(code, 16)


def sizes(lists, cap):
    found = []
    base = 0
    for kind in range(2):
        chunk = kind * (lists.shape[0] // 2)
        n = lists[chunk, 1, 0]
        held = jnp.minimum(n, jnp.maximum(cap - base, 0))
        found.append((n, lists[chunk, 1, 1], held, base))
        base = base + held
    return found


def gather(refs, target, sems):
    run = target.shape[0] // len(refs)
    return [pltpu.make_async_copy(ref, target.at[pl.ds(p * run, run)], sems.at[p]) for p, ref in enumerate(refs)]


def tiles_kernel(pieces, per_device, cap, *refs):
    list_ref, tile_ref = refs[pieces : pieces + 2]
    cloud, stage, plan, lists, sems, list_sems = refs[pieces + 2 :]
    devices = cloud.shape[0]
    blocks = devices * per_device
    copies = gather(refs[:pieces], cloud, sems)
    for copy in copies:
        copy.start()
    for copy in copies:
        copy.wait()

    cols = lax.axis_size("col")
    col_id = lax.axis_index("col")
    mine = lax.axis_index("row") * cols + (col_id & 1) * (cols // 2) + lax.shift_right_logical(col_id, 1)
    mine = mine * per_device
    ids = lax.broadcasted_iota(jnp.int32, (blocks, LANES), 0)
    batch = 8

    def one_hot(device, line):
        row = cloud[device, 3, line : line + 1, 0:LANES].astype(jnp.int32)
        row = jnp.where(row >= 0, row ^ mine, -1)
        return jnp.where(ids == row, 1.0, 0.0).astype(jnp.bfloat16)

    def pairs_of(group):
        sides = [
            jnp.concatenate([one_hot(group * batch + k, line) for k in range(batch)], axis=1) for line in range(2)
        ]
        return lax.dot_general(*sides, (((1,), (1,)), ((), ())), preferred_element_type=jnp.float32)

    stage[...] = pairs_of(0)

    def add_pairs(group, carry):
        stage[...] += pairs_of(group)
        return carry

    lax.fori_loop(1, devices // batch, add_pairs, 0)

    boxes = cloud[:, 3, :, LANES : 2 * LANES].reshape(blocks, LANES)
    flat = jnp.transpose(boxes)
    extent = jnp.max(flat[3:6, :] - flat[0:3, :])
    apart = None
    for axis in range(3):
        gap = jnp.maximum(
            boxes[:, axis : axis + 1] - flat[3 + axis : 4 + axis, :],
            flat[axis : axis + 1, :] - boxes[:, 3 + axis : 4 + axis],
        )
        gap = jnp.maximum(gap, 0.0)
        apart = gap * gap if apart is None else apart + gap * gap
    stage[...] = jnp.where(apart < 1.0001, stage[...], 0.0)

    listed = stage[...] > 0.0
    rows = lax.broadcasted_iota(jnp.int32, (blocks, blocks), 0)
    columns = lax.broadcasted_iota(jnp.int32, (blocks, blocks), 1)
    near_row = jnp.max(stage[0:per_device, :], axis=0, keepdims=True) > 0.0
    near_row = near_row | (lax.broadcasted_iota(jnp.int32, (1, blocks), 1) < per_device)
    near_col = jnp.max(stage[:, 0:per_device], axis=1, keepdims=True) > 0.0
    near_col = near_col | (lax.broadcasted_iota(jnp.int32, (blocks, 1), 0) < per_device)

    def counted(left, right):
        return jnp.dot(left.astype(jnp.bfloat16), right.astype(jnp.bfloat16), preferred_element_type=jnp.float32)

    low_ids = lax.broadcasted_iota(jnp.int32, (blocks, CHUNK), 0).astype(jnp.float32)
    lower = jnp.where(rows >= columns, 1.0, 0.0)
    upper = jnp.where(rows < columns, 1.0, 0.0)

    def write_list(kind, used):
        rank = counted(lower, used)
        count = rank[blocks - 1 : blocks, :]
        start = jnp.sum(counted(used, upper), axis=0, keepdims=True)
        both = jnp.concatenate([start, start + count, jnp.zeros((6, blocks), jnp.float32)], axis=0)
        both = jnp.transpose(both)
        start_col = both[:, 0:1]
        stop_col = both[:, 1:2]
        n = jnp.sum(count).astype(jnp.int32)
        own = lax.broadcasted_iota(jnp.int32, (1, blocks), 1) < per_device
        n_own = jnp.sum(jnp.where(own, count, 0.0)).astype(jnp.int32)
        stage[...] = rank * used
        lane = lax.broadcasted_iota(jnp.int32, (1, CHUNK), 1)
        totals = jnp.where(lane == 0, n, n_own)
        first = kind * (list_ref.shape[0] // 2)

        def write(chunk, place_in_plan):
            place = lane.astype(jnp.float32) + chunk * float(CHUNK)
            pick = jnp.where((start_col <= place) & (place < stop_col), 1.0, 0.0)
            column = jnp.sum(pick * low_ids, axis=0, keepdims=True)
            begin = jnp.sum(pick * start_col, axis=0, keepdims=True)
            high, low = split(stage[...])
            ranks = counted(high, pick) + counted(low, pick)
            match = jnp.where(ranks == place - begin + 1.0, 1.0, 0.0)
            row = jnp.sum(match * low_ids, axis=0, keepdims=True)
            code = row.astype(jnp.int32) * 65536 + column.astype(jnp.int32)
            plan[place_in_plan] = jnp.concatenate([code, totals], axis=0)

        def send(chunk, place_in_plan):
            return [
                pltpu.make_async_copy(plan.at[place_in_plan], target.at[first + chunk], list_sems.at[place_in_plan, k])
                for k, target in enumerate((lists, list_ref))
            ]

        def write_more(chunk, carry):
            write(chunk.astype(jnp.float32), 2)
            for copy in send(chunk, 2):
                copy.start()
            for copy in send(chunk, 2):
                copy.wait()
            return carry

        write(0.0, kind)
        for copy in send(0, kind):
            copy.start()
        lax.fori_loop(1, (n + CHUNK - 1) // CHUNK, write_more, 0)
        return send(0, kind)

    sent = [
        write_list(0, jnp.where(listed & (rows > columns) & near_row & near_col, 1.0, 0.0)),
        write_list(1, jnp.where(listed & near_row & ((rows == columns) | jnp.logical_not(near_col)), 1.0, 0.0)),
    ]
    for to_lists, _ in sent:
        to_lists.wait()
    kinds = sizes(lists, cap)

    first_held = kinds[0][2]
    held = first_held + kinds[1][2]

    def write_tiles(form):
        def body(group, carry):
            for part in range(BATCH):
                slot = group * BATCH + part
                kind = (slot >= first_held).astype(jnp.int32)
                i, j = entry(lists, kind, slot - kind * first_held)
                form(point_rows(cloud, i, per_device), point_rows(cloud, j, per_device), tile_ref.at[slot])
            return carry

        lax.fori_loop(0, (held + BATCH - 1) // BATCH, body, 0)

    @pl.when(extent <= 1.5 / support)
    def _():
        write_tiles(evaluate_flat)

    @pl.when(extent > 1.5 / support)
    def _():
        write_tiles(evaluate)

    for _, to_result in sent:
        to_result.wait()


def apply_kernel(pieces, point_pieces, per_device, cap, list_ref, tile_ref, *refs):
    value_refs = refs[:pieces]
    point_refs = refs[pieces : pieces + point_pieces]
    w_ref, x_ref, moment_ref = refs[pieces + point_pieces : pieces + point_pieces + 3]
    field, total, second, late, cloud, lists, sems, point_sems, list_sem = refs[pieces + point_pieces + 3 :]
    devices = field.shape[0]
    blocks = devices * per_device
    block_shift = per_device.bit_length() - 1
    low_mask = per_device - 1
    fills = [pltpu.make_async_copy(list_ref, lists, list_sem)] + gather(value_refs, field, sems)
    for copy in fills:
        copy.start()
    total[...] = jnp.zeros_like(total)
    for copy in fills:
        copy.wait()
    kinds = sizes(lists, cap)

    def at(b):
        return lax.shift_right_logical(b, block_shift), pl.ds(2 * (b & low_mask), 2)

    def product(vector, tile, contract):
        high, low = split(4.0 * vector)
        both = jnp.concatenate([high, low], axis=0)
        dims = (((1,), (contract,)), ((), ()))
        first = lax.dot_general(both, tile[0], dims, preferred_element_type=jnp.float32)
        later = lax.dot_general(high, tile[1], dims, preferred_element_type=jnp.float32)
        return (first[0:16] + first[16:32] + later).reshape(2, 8, BLK)

    def load(ref, b):
        device, span = at(b)
        return ref[device, span].reshape(16, BLK)

    def add(ref, b, value):
        device, span = at(b)
        ref[device, span] += value

    def image(b):
        return load(total, b) + load(field, b)

    def run(kind, held, source, target, spare, back):
        base = kinds[kind][3]

        def body(group, carry):
            pending = []
            for u in range(GROUP):
                k = group * GROUP + u
                i, j = entry(lists, kind, k)
                live = k < held
                pending.append((jnp.where(live, i, spare), product(source(j), tile_ref.at[base + k], 0)))
                if back == "always":
                    pending.append((jnp.where(live, j, spare), product(source(i), tile_ref.at[base + k], 1)))
            for b, value in pending:
                add(target, b, value)
            if back == "some":
                for u in range(GROUP):
                    k = group * GROUP + u
                    i, j = entry(lists, kind, k)

                    @pl.when((k < held) & (j < spare))
                    def _():
                        add(target, j, product(source(i), tile_ref.at[base + k], 1))

            return carry

        lax.fori_loop(0, (held + GROUP - 1) // GROUP, body, 0)

    def run_late(kind, first, last, source, target, spare):
        def body(k, carry):
            i, j = entry(lists, kind, k)
            evaluate(point_rows(cloud, i, per_device), point_rows(cloud, j, per_device), late)
            add(target, i, product(source(j), late, 0))
            if kind == 0:

                @pl.when(j < spare)
                def _():
                    add(target, j, product(source(i), late, 1))

            return carry

        lax.fori_loop(first, last, body, 0)

    def own_field(b):
        return load(field, b)

    run(0, kinds[0][2], own_field, total, blocks, "always")
    run(1, kinds[1][2], own_field, total, blocks, "never")

    @pl.when((kinds[0][0] > kinds[0][2]) | (kinds[1][0] > kinds[1][2]))
    def _():
        copies = gather(point_refs, cloud, point_sems)
        for copy in copies:
            copy.start()
        for copy in copies:
            copy.wait()
        for kind, (n, _, held, _) in enumerate(kinds):
            run_late(kind, held, n, own_field, total, blocks)

    second[0] = total[0] + field[0]
    for kind, back in enumerate(("some", "never")):
        _, n_own, held, _ = kinds[kind]
        held_own = jnp.minimum(n_own, held)
        run(kind, held_own, image, second, per_device, back)
        run_late(kind, held_own, n_own, image, second, per_device)

    v = field[0].reshape(per_device, 16, BLK)
    w = (total[0] + field[0]).reshape(per_device, 16, BLK)
    x = second[0].reshape(per_device, 16, BLK)
    w_ref[...] = w
    x_ref[...] = x

    def over(values):
        return jnp.sum(jnp.sum(values, axis=0), axis=1, keepdims=True)

    vv = over(v * v)
    vw = over(v * w)
    shift = jnp.where(vw != 0.0, vv / jnp.where(vw != 0.0, vw, 1.0), 0.0)
    q = v - shift[None] * w
    s = w - shift[None] * x
    sums = [shift, over(q * q), over(q * w), over(w * w), over(q * s), over(w * s + q * x), over(w * x)]
    lane = lax.broadcasted_iota(jnp.int32, (16, LANES), 1)
    sent = jnp.zeros((16, LANES), jnp.float32)
    for m, value in enumerate(sums):
        sent = jnp.where(lane == m, value, sent)
    sent = jnp.concatenate([sent, jnp.zeros((LANES - 16, LANES), jnp.float32)], axis=0)
    sent = jnp.transpose(sent)[0:8]
    for device in range(devices):
        moment_ref[device] = sent


def finish_kernel(per_device, moment_ref, values_ref, w_ref, x_ref, solution_ref, residual_ref):
    def take(m):
        return moment_ref[:, m, :]

    def whole(values):
        return jnp.sum(values, axis=0, keepdims=True)

    shift, qq, qw, ww = take(SHIFT), take(QQ), take(QW), take(WW)
    rr = whole(qq + 2.0 * shift * qw + shift * shift * ww)
    vw = whole(qw + shift * ww)
    alpha = rr / vw
    delta = alpha - shift
    fresh = whole(qq - 2.0 * delta * qw + delta * delta * ww)
    mixed = whole(qw - delta * ww)
    curve = whole(take(QS) - delta * take(CROSS) + delta * delta * take(WX))
    beta = fresh / rr
    curve = curve + 2.0 * beta * mixed + beta * beta * vw
    again = fresh / curve
    steps = jnp.transpose(jnp.concatenate([alpha, beta, again, jnp.zeros((5, LANES), jnp.float32)], axis=0))
    for half in range(2):
        lines = slice(8 * half, 8 * half + 8)
        alpha, beta, again = (steps[lines, m : m + 1] for m in range(3))
        for b in range(per_device):
            at = (lines, slice(b * BLK, (b + 1) * BLK))
            v = values_ref[at]
            w = w_ref[b, lines, :]
            x = x_ref[b, lines, :]
            r = v - alpha * w
            d = r + beta * v
            solution_ref[at] = alpha * v + again * d
            residual_ref[at] = r - again * (w - alpha * x + beta * w)


def local(points, values, tile_lists):
    fields, owned_points = values.shape
    per_device = owned_points // BLK
    rows = lax.axis_size("row")
    cols = lax.axis_size("col")
    devices = rows * cols
    depth = cols // 2
    vmem = pl.BlockSpec(memory_space=pltpu.VMEM)
    anywhere = pl.BlockSpec(memory_space=pl.ANY)
    height = 2 * per_device
    blocks = devices * per_device

    own_values, own_points = pl.pallas_call(
        functools.partial(pack_kernel, per_device),
        out_shape=(
            jax.ShapeDtypeStruct((height, 8, BLK), jnp.float32),
            jax.ShapeDtypeStruct((4, per_device, BLK), jnp.float32),
        ),
        in_specs=[vmem, vmem, vmem],
        out_specs=(vmem, vmem),
        name="pack",
    )(values, points, tile_lists)

    def swap(array, row_mask, col_mask):
        if row_mask == 0:
            return lax.ppermute(array, "col", [(i, i ^ col_mask) for i in range(cols)])
        if col_mask == 0:
            return lax.ppermute(array, "row", [(i, i ^ row_mask) for i in range(rows)])
        pairs = [
            (r * cols + c, (r ^ row_mask) * cols + (c ^ col_mask)) for r in range(rows) for c in range(cols)
        ]
        return lax.ppermute(array, ("row", "col"), pairs)

    def along(array):
        return jnp.stack([array] + [swap(array, 0, 2 * z) for z in range(1, depth)])

    def across(line):
        return {
            (row_mask, x): swap(line, row_mask, x) if (row_mask, x) != (0, 0) else line
            for row_mask, x in itertools.product(range(0, rows, 2), range(2))
        }

    def pairs(plane):
        plane = dict(plane)
        for (row_mask, x), part in list(plane.items()):
            plane[row_mask + 1, x] = swap(part, 1, 0)
        return [plane[row_mask, x] for row_mask in range(rows) for x in range(2)]

    point_plane = across(along(own_points))
    value_line, point_plane = lax.optimization_barrier((along(own_values), point_plane))
    point_parts = pairs(point_plane)
    value_plane = across(value_line)
    core_line = swap(value_line, 1, 0)

    chunks = (devices * tile_lists.shape[1] + CHUNK - 1) // CHUNK
    tile_bytes = 4 * BLK * BLK
    cloud_bytes = devices * 4 * per_device * BLK * 4
    field_bytes = blocks * fields * BLK * 4
    tiles_limit = cloud_bytes + 6 * 4 * blocks * blocks + 10 * 2**20
    apply_limit = cloud_bytes + 2 * field_bytes + 6 * 2**20
    room = 60 * 2**20 - max(GROUP, BATCH) * tile_bytes - max(tiles_limit, apply_limit)
    cap = max(GROUP, min(112, room // tile_bytes // GROUP * GROUP))
    lists, tiles = pl.pallas_call(
        functools.partial(tiles_kernel, len(point_parts), per_device, cap),
        out_shape=(
            pltpu.HBM((2 * chunks, 2, CHUNK), jnp.int32),
            pltpu.VMEM((cap + max(GROUP, BATCH), 2, BLK, BLK), jnp.bfloat16),
        ),
        in_specs=[anywhere] * len(point_parts),
        out_specs=(anywhere, vmem),
        scratch_shapes=[
            pltpu.VMEM((devices, 4, per_device, BLK), jnp.float32),
            pltpu.VMEM((blocks, blocks), jnp.float32),
            pltpu.VMEM((3, 2, CHUNK), jnp.int32),
            pltpu.SMEM((2 * chunks, 2, CHUNK), jnp.int32),
            pltpu.SemaphoreType.DMA((len(point_parts),)),
            pltpu.SemaphoreType.DMA((3, 2)),
        ],
        compiler_params=pltpu.CompilerParams(vmem_limit_bytes=tiles_limit),
        cost_estimate=pl.CostEstimate(flops=10**9, bytes_accessed=30 * 2**20, transcendentals=10**7),
        name="tiles",
    )(*point_parts)
    value_plane.pop((0, 0))
    value_plane, lists, tiles = lax.optimization_barrier((value_plane, lists, tiles))
    value_parts = [value_line, None, core_line, None] + [None] * (2 * rows - 4)
    for (row_mask, x), part in value_plane.items():
        value_parts[2 * row_mask + x] = part
        value_parts[2 * row_mask + 2 + x] = swap(part, 1, 0)
    block_shape = jax.ShapeDtypeStruct((per_device, fields, BLK), jnp.float32)
    w, x, moments = pl.pallas_call(
        functools.partial(apply_kernel, len(value_parts), len(point_parts), per_device, cap),
        out_shape=(block_shape, block_shape, jax.ShapeDtypeStruct((devices, 8, LANES), jnp.float32)),
        in_specs=[anywhere, vmem] + [anywhere] * (len(value_parts) + len(point_parts)),
        out_specs=(vmem, vmem, vmem),
        scratch_shapes=[
            pltpu.VMEM((devices, height, 8, BLK), jnp.float32),
            pltpu.VMEM((devices + 1, height, 8, BLK), jnp.float32),
            pltpu.VMEM((2, height, 8, BLK), jnp.float32),
            pltpu.VMEM((2, BLK, BLK), jnp.bfloat16),
            pltpu.VMEM((devices, 4, per_device, BLK), jnp.float32),
            pltpu.SMEM((2 * chunks, 2, CHUNK), jnp.int32),
            pltpu.SemaphoreType.DMA((len(value_parts),)),
            pltpu.SemaphoreType.DMA((len(point_parts),)),
            pltpu.SemaphoreType.DMA,
        ],
        compiler_params=pltpu.CompilerParams(vmem_limit_bytes=apply_limit),
        name="apply",
    )(
        pltpu.with_memory_space_constraint(lists, pltpu.HBM),
        pltpu.with_memory_space_constraint(tiles, pltpu.VMEM),
        *value_parts,
        *point_parts,
    )
    moments = lax.all_to_all(moments, ("row", "col"), 0, 0, tiled=False)
    return pl.pallas_call(
        functools.partial(finish_kernel, per_device),
        out_shape=(jax.ShapeDtypeStruct(values.shape, jnp.float32),) * 2,
        in_specs=[vmem] * 4,
        out_specs=(vmem, vmem),
        name="finish",
    )(moments, values, w, x)


def solution(mesh):
    placed = (P(None, ("row", "col")), P(None, ("row", "col")), P(None, ("row", "col")))
    return jax.shard_map(
        local,
        mesh=mesh,
        in_specs=placed,
        out_specs=(P(None, ("row", "col")), P(None, ("row", "col"))),
        check_vma=False,
    )
```
